32 devices in a mesh: grp: 8 (over z, core), blk: 4 (over y, x).
Axes of the slice: x: 2, y: 2, z: 4, core: 2. Of those that a mesh axis runs over, the one named last changes fastest.
Arguments:
- temp: float32 [8, 512, 512], P(None, 'grp', 'blk'), may hold values from -6 to 6
- uvel: float32 [8, 512, 512], P(None, 'grp', 'blk'), may hold values from -0.4 to 0.4
- vvel: float32 [8, 512, 512], P(None, 'grp', 'blk'), may hold values from -0.4 to 0.4
- couple_col: int32 [8, 4, 2048], P('grp', 'blk'), may hold values from 0 to 8191
- couple_cell: int32 [8, 4, 2048], P('grp', 'blk'), may hold values from 0 to 524287
- cavity: int32 [8, 4, 2048], P('grp', 'blk'), may hold values 0 or 1
- thickness: float32 [512, 1024], P('blk'), may hold values from 0.2 to 2
- viscosity: float32 [512, 1024], P('blk'), may hold values from 0.5 to 4
- friction: float32 [512, 1024], P('blk'), may hold values from 0.02 to 0.3
- drive: float32 [512, 1024], P('blk'), may hold values from -6 to 6
Outputs:
- temp_new: float32 [8, 512, 512], P(None, 'grp', 'blk')
- ice_velocity: float32 [512, 1024], P('blk')
The draws below stay inside these ranges and needn't reach their ends.
Inputs may be any that keep to these rules, and one draw needn't show every extreme that they name: `couple_col`: an index of a column within the 64 x 128 block of the device holding the entry, row-major. `couple_cell`: a row-major index into the whole ice grid.
All inputs are finite; a program needn't handle non-finite values. No bound on the sum of `cavity` on one device may be relied on, other than what follows from the above.
Results may differ from the reference program's by a relative error of at most 0.0003.
Values sent between devices are 32-bit elements; how exact they have to be, the bound alone decides.
A program may use at most 64 MiB of HBM per device.

```python
import math
import jax
import jax.numpy as jnp
from jax import lax

LEV = 8
CX = 64
CY = 128
CIX = 128
IY = 1024
COUPLE = 2048
LEVELS = 3
SMOOTH_SWEEPS = 2
COARSE_SWEEPS = 4
CYCLES = 2
OX = 512
OY = 512
NIX = 512
NI = 524288
N_GRP = 8
N_BLK = 4


def touch_ends(entries, rng, least, top_value):
    spot = [jax.random.randint(jax.random.fold_in(rng, axis), (), 0, length) for axis, length in enumerate(entries.shape)]
    longest = entries.shape.index(max(entries.shape))
    neighbour = spot[:longest] + [(spot[longest] + 1) % entries.shape[longest]] + spot[longest + 1:]
    return entries.at[tuple(spot)].set(least).at[tuple(neighbour)].set(top_value)


def level_of(key, extent, cuts, smallest, high):
    level = 1.0
    for dim, parts in cuts:
        steps = jax.random.uniform(jax.random.fold_in(jax.random.fold_in(key, 6), dim), (parts,), jnp.float32, smallest / len(cuts), high / len(cuts))
        level = level * jnp.repeat(jnp.exp(steps), extent[dim] // parts).reshape((-1,) + (1,) * (len(extent) - 1 - dim))
    return level


def bell_draw(own_key, dims, deviation, most, pieces=(), kind=jnp.bfloat16):
    entries = deviation * jax.random.normal(own_key, dims, jnp.float32)
    if pieces:
        entries = entries * level_of(own_key, dims, pieces, -0.22, 0.18)
    return jnp.clip(entries, -most, most).astype(kind)


def setup_inputs(seed: int = 0) -> dict:
    keys = jax.random.split(jax.random.key(seed), 11)
    return {
        "temp": bell_draw(keys[0], (LEV, OX, OY), 1.0, 6.0, ((1, 8), (2, 4)), jnp.float32),
        "uvel": jnp.clip(jax.random.uniform(keys[1], (LEV, OX, OY), jnp.float32, -0.4, 0.4) * level_of(keys[1], (LEV, OX, OY), ((1, 8), (2, 4)), -0.4, 0.0), -0.4, 0.4),
        "vvel": jnp.clip(jax.random.uniform(keys[2], (LEV, OX, OY), jnp.float32, -0.4, 0.4) * level_of(keys[2], (LEV, OX, OY), ((1, 8), (2, 4)), -0.4, 0.0), -0.4, 0.4),
        "couple_col": touch_ends(jax.random.randint(keys[3], (N_GRP, N_BLK, COUPLE), 0, CX * CY), jax.random.fold_in(keys[3], 1), 0, (CX * CY) - 1).astype(jnp.int32),
        "couple_cell": touch_ends(jax.random.randint(keys[4], (N_GRP, N_BLK, COUPLE), 0, NI), jax.random.fold_in(keys[4], 1), 0, NI - 1).astype(jnp.int32),
        "cavity": touch_ends((jax.random.randint(keys[5], (N_GRP, N_BLK, COUPLE), 0, 2) < 1).astype(jnp.int32), jax.random.fold_in(keys[5], 1), 0, 1),
        "thickness": jnp.clip(0.2 + 1.8 * jax.random.uniform(keys[6], (NIX, IY), jnp.float32) ** level_of(keys[6], (NIX, IY), ((0, 4),), -0.2, 0.2), 0.2, 2.0),
        "viscosity": jnp.clip(jnp.exp(math.log(4.0) - 2.0794415 * jax.random.uniform(keys[7], (NIX, IY), jnp.float32) ** level_of(keys[7], (NIX, IY), ((0, 4),), -0.2, 0.2)), 0.5, 4.0),
        "friction": jnp.clip(jnp.exp(math.log(0.3) - 2.7080503 * jax.random.uniform(keys[8], (NIX, IY), jnp.float32) ** level_of(keys[8], (NIX, IY), ((0, 4),), -0.2, 0.2)), 0.02, 0.3),
        "drive": bell_draw(keys[9], (NIX, IY), 1.0, 6.0, ((0, 4),), jnp.float32),
    }


omega = 0.8
kappa = 0.1
vertical_mix = 0.2
melt_rate = 0.5


def face_terms(visc_pad, friction, scale):
    center = visc_pad[1:-1, 1:-1]
    east = 0.5 * (center + visc_pad[2:, 1:-1]) * scale
    west = 0.5 * (center + visc_pad[:-2, 1:-1]) * scale
    north = 0.5 * (center + visc_pad[1:-1, 2:]) * scale
    south = 0.5 * (center + visc_pad[1:-1, :-2]) * scale
    diagonal = east + west + north + south + friction
    return (east, west, north, south, diagonal)


def apply_padded(field_pad, terms):
    east, west, north, south, diagonal = terms
    field = field_pad[1:-1, 1:-1]
    return (diagonal * field - east * field_pad[2:, 1:-1] - west * field_pad[:-2, 1:-1]
            - north * field_pad[1:-1, 2:] - south * field_pad[1:-1, :-2])


def restrict(field):
    paired = field[0::2] + field[1::2]
    return 0.25 * (paired[:, 0::2] + paired[:, 1::2])


def prolong(field):
    rows, cols = field.shape
    expand = (jnp.arange(2 * cols)[None, :] // 2 == jnp.arange(cols)[:, None]).astype(jnp.float32)
    wide = jnp.dot(field, expand, precision=lax.Precision.HIGHEST)
    return jnp.broadcast_to(wide[:, None, :], (rows, 2, 2 * cols)).reshape(2 * rows, 2 * cols)


def vcycle(depth, field, source, terms_list, operate):
    terms = terms_list[depth]
    sweeps = COARSE_SWEEPS if depth == LEVELS - 1 else SMOOTH_SWEEPS
    for sweep_index in range(sweeps):
        field = field + omega * (source - operate(field, terms)) / terms[4]
    if depth == LEVELS - 1:
        return field
    residual = source - operate(field, terms)
    coarse_source = restrict(residual)
    coarse = vcycle(depth + 1, jnp.zeros_like(coarse_source), coarse_source, terms_list, operate)
    field = field + prolong(coarse)
    for sweep_index in range(SMOOTH_SWEEPS):
        field = field + omega * (source - operate(field, terms)) / terms[4]
    return field


def ocean_tendency(temp_pad, uvel_pad, vvel_pad):
    temp = temp_pad[:, 1:-1, 1:-1]
    uvel = uvel_pad[:, 1:-1, 1:-1]
    vvel = vvel_pad[:, 1:-1, 1:-1]
    east_speed = 0.5 * (uvel + uvel_pad[:, 2:, 1:-1])
    flux_east = jnp.maximum(east_speed, 0.0) * temp + jnp.minimum(east_speed, 0.0) * temp_pad[:, 2:, 1:-1]
    west_speed = 0.5 * (uvel + uvel_pad[:, :-2, 1:-1])
    flux_west = jnp.maximum(west_speed, 0.0) * temp_pad[:, :-2, 1:-1] + jnp.minimum(west_speed, 0.0) * temp
    north_speed = 0.5 * (vvel + vvel_pad[:, 1:-1, 2:])
    flux_north = jnp.maximum(north_speed, 0.0) * temp + jnp.minimum(north_speed, 0.0) * temp_pad[:, 1:-1, 2:]
    south_speed = 0.5 * (vvel + vvel_pad[:, 1:-1, :-2])
    flux_south = jnp.maximum(south_speed, 0.0) * temp_pad[:, 1:-1, :-2] + jnp.minimum(south_speed, 0.0) * temp
    laplace = (temp_pad[:, 2:, 1:-1] + temp_pad[:, :-2, 1:-1] + temp_pad[:, 1:-1, 2:]
               + temp_pad[:, 1:-1, :-2] - 4.0 * temp)
    between = temp[1:] - temp[:-1]
    zero_layer = jnp.zeros_like(temp[:1])
    vert = jnp.concatenate([between, zero_layer], axis=0) - jnp.concatenate([zero_layer, between], axis=0)
    return temp + flux_west - flux_east + flux_south - flux_north + kappa * laplace + vertical_mix * vert


def operate_whole(field, terms):
    return apply_padded(jnp.pad(field, 1), terms)


def reference(temp, uvel, vvel, couple_col, couple_cell, cavity, thickness, viscosity, friction, drive):
    blocks = N_GRP * N_BLK
    top = temp[0].reshape(N_GRP, CX, N_BLK, CY).transpose(0, 2, 1, 3).reshape(blocks, CX * CY)
    columns = couple_col.reshape(blocks, COUPLE)
    cells = couple_cell.reshape(-1)
    top_entry = jnp.take_along_axis(top, columns, axis=1).reshape(-1)
    draft = thickness.reshape(-1)[cells]
    melt = cavity.reshape(-1).astype(jnp.float32) * melt_rate * (top_entry + 0.5 + 0.5 * draft)

    def column_sum(values, positions):
        return jax.ops.segment_sum(values, positions, CX * CY)

    column_melt = jax.vmap(column_sum)(melt.reshape(blocks, COUPLE), columns)
    surface = column_melt.reshape(N_GRP, N_BLK, CX, CY).transpose(0, 2, 1, 3).reshape(N_GRP * CX, N_BLK * CY)
    padded = jnp.pad(jnp.stack([temp, uvel, vvel]), ((0, 0), (0, 0), (1, 1), (1, 1)))
    stepped = ocean_tendency(padded[0], padded[1], padded[2])
    temp_new = jnp.concatenate([stepped[:1] - melt_rate * surface[None], stepped[1:]], axis=0)

    melt_ice = jax.ops.segment_sum(melt, cells, N_BLK * CIX * IY).reshape(N_BLK * CIX, IY)
    source = drive + melt_ice
    terms_list = []
    visc = viscosity
    fric = friction
    for depth in range(LEVELS):
        terms_list.append(face_terms(jnp.pad(visc, 1), fric, 0.25 ** depth))
        if depth + 1 < LEVELS:
            visc = restrict(visc)
            fric = restrict(fric)
    field = jnp.zeros_like(source)
    for cycle_index in range(CYCLES):
        field = vcycle(0, field, source, terms_list, operate_whole)
    return temp_new, field
```

```python
import functools

import jax
import jax.numpy as jnp
from jax import lax
from jax.experimental import pallas as pl
from jax.experimental.pallas import tpu as pltpu
from jax.sharding import PartitionSpec as P

LEVELS = 3
SMOOTH_SWEEPS = 2
COARSE_SWEEPS = 4
CYCLES = 2

omega = 0.8
kappa = 0.1
vertical_mix = 0.2
melt_rate = 0.5

MESH = pl.DeviceIdType.MESH
VM = pl.BlockSpec(memory_space=pltpu.VMEM)
LIMIT = 56 * 1024 * 1024
F32 = jnp.float32
BF16 = jnp.bfloat16


def split(x):
    high = x.astype(BF16).astype(F32)
    return high, x - high


def dot2(x, one, left=False):
    out = None
    for part in split(x):
        part = part.astype(BF16)
        term = jnp.dot(one, part, preferred_element_type=F32) if left else jnp.dot(
            part, one, preferred_element_type=F32)
        out = term if out is None else out + term
    return out


def nt(a, b):
    return lax.dot_general(a, b, (((1,), (1,)), ((), ())), preferred_element_type=F32)


def iota(shape, dim):
    return lax.broadcasted_iota(jnp.int32, shape, dim)


def remote(src, dst, send, recv, device):
    return pltpu.make_async_remote_copy(
        src_ref=src, dst_ref=dst, send_sem=send, recv_sem=recv, device_id=device,
        device_id_type=MESH)


def couple_kernel(n_grp, n_blk, temp0, col, cell, cav, thick, visc, fric, row_edge, col_edge,
                  part_out, draft_out, top_out, visc_out, fric_out, row_out, col_out,
                  ent_cell, ent_cav, ent_w, acc, dsem_s, dsem_r, hsem_s, hsem_r):
    g = lax.axis_index("grp")
    b = lax.axis_index("blk")
    core = lax.rem(g, 2)
    rows, cols = thick.shape
    count = cell.shape[1]
    half = rows // 2
    up_g, dn_g = lax.rem(g + 1, n_grp), lax.rem(g + n_grp - 1, n_grp)
    up_b, dn_b = lax.rem(b + 1, n_blk), lax.rem(b + n_blk - 1, n_blk)

    barrier = pltpu.get_barrier_semaphore()
    peers = [(g, lax.rem(b + k, n_blk)) for k in range(1, n_blk)]
    for device in peers + [(up_g, b), (dn_g, b)]:
        pl.semaphore_signal(barrier, inc=1, device_id=device, device_id_type=MESH)
    pl.semaphore_wait(barrier, n_blk + 1)

    ent = []
    for k in range(1, n_blk):
        target = peers[k - 1]
        trio = [
            remote(cell, ent_cell.at[k - 1], dsem_s.at[k - 1, 0], dsem_r.at[k - 1, 0], target),
            remote(cav, ent_cav.at[k - 1], dsem_s.at[k - 1, 1], dsem_r.at[k - 1, 1], target),
            remote(ent_w.at[0], ent_w.at[k], dsem_s.at[k - 1, 2], dsem_r.at[k - 1, 2], target),
        ]
        trio[0].start()
        trio[1].start()
        ent.append(trio)

    ids = col[...]
    ocean_rows, ocean_cols = temp0.shape
    row = ids // ocean_cols
    lane = ids - row * ocean_cols
    pick = (iota((ocean_cols, count), 0) == lane).astype(F32).astype(BF16)
    wide = dot2(temp0[...], pick)
    low = temp0[...] - split(temp0[...])[0]
    rest = split(low)[1]
    wide = wide + jnp.dot(rest.astype(BF16), pick, preferred_element_type=F32)
    top = jnp.sum(jnp.where(iota((ocean_rows, count), 0) == row, wide, 0.0), axis=0, keepdims=True)
    top_out[...] = top
    ent_w[0] = cav[...].astype(F32) * melt_rate * (top + 0.5)
    for trio in ent:
        trio[2].start()

    edges = [
        remote(row_edge.at[1], row_out.at[0], hsem_s.at[0], hsem_r.at[0], (up_g, b)),
        remote(row_edge.at[0], row_out.at[1], hsem_s.at[1], hsem_r.at[1], (dn_g, b)),
        remote(col_edge.at[1], col_out.at[0], hsem_s.at[2], hsem_r.at[2], (g, up_b)),
        remote(col_edge.at[0], col_out.at[1], hsem_s.at[3], hsem_r.at[3], (g, dn_b)),
    ]
    for copy in edges:
        copy.start()
    own = pl.multiple_of((1 - core) * half, 8)
    halo = pl.multiple_of(core * 2 * half, 8)
    target = (g, lax.rem(b + n_blk + 1 - 2 * core, n_blk))
    does = jnp.where(core == 0, b < n_blk - 1, b > 0)
    gets = jnp.where(core == 0, b > 0, b < n_blk - 1)
    ice = [
        remote(visc.at[pl.ds(own, half)], visc_out.at[pl.ds(halo, half)], hsem_s.at[4],
               hsem_r.at[4], target),
        remote(fric.at[pl.ds(own, half)], fric_out.at[pl.ds(halo, half)], hsem_s.at[5],
               hsem_r.at[5], target),
    ]

    @pl.when(does)
    def _():
        for copy in ice:
            copy.start()

    inside = pl.multiple_of((1 - core) * half, 8)
    visc_out[pl.ds(inside, 2 * half), :] = visc[...]
    fric_out[pl.ds(inside, 2 * half), :] = fric[...]

    @pl.when(jnp.logical_not(gets))
    def _():
        visc_out[pl.ds(halo, half), :] = jnp.zeros((half, cols), F32)
        fric_out[pl.ds(halo, half), :] = jnp.ones((half, cols), F32)

    high, low = split(thick[...])
    thick2 = jnp.concatenate([high, low], axis=0).astype(BF16)
    acc[...] = jnp.zeros_like(acc)
    chunk = 512
    for k in range(n_blk):
        if k > 0:
            for copy in ent[k - 1]:
                copy.wait_recv()
        cells_ref = cell if k == 0 else ent_cell.at[k - 1]
        cav_ref = cav if k == 0 else ent_cav.at[k - 1]

        for part in range(count // chunk):
            at = slice(part * chunk, (part + 1) * chunk)
            cells = cells_ref[:, at]
            grid_row = cells // cols
            lane = cells - grid_row * cols
            hit = iota((rows, chunk), 0) == grid_row - b * rows
            pick = (iota((cols, chunk), 0) == lane).astype(F32).astype(BF16)
            w_high, w_low = split(ent_w[k, :, at])
            spread = jnp.concatenate(
                [
                    jnp.where(hit, w_high, 0.0).astype(BF16),
                    jnp.where(hit, w_low, 0.0).astype(BF16),
                    jnp.where(hit, cav_ref[:, at].astype(F32), 0.0).astype(BF16),
                ], axis=0)
            acc[...] += nt(spread, pick)
            drafts = jnp.dot(thick2, pick, preferred_element_type=F32)
            draft_out[k, :, at] = jnp.sum(
                jnp.where(hit, drafts[:rows] + drafts[rows:], 0.0), axis=0, keepdims=True)

    part_out[...] = acc[:rows] + acc[rows:2 * rows] + (0.5 * melt_rate) * acc[2 * rows:] * thick[...]

    for trio in ent:
        for copy in trio:
            copy.wait_send()
    for copy in edges:
        copy.wait()

    @pl.when(does)
    def _():
        for copy in ice:
            copy.wait_send()

    @pl.when(gets)
    def _():
        for copy in ice:
            copy.wait_recv()


def reduce_kernel(n_grp, n_blk, part, drive, drafts, source, draft_out,
                  near, pair, far, dback, sem_s, sem_r, dsem_s, dsem_r):
    g = lax.axis_index("grp")
    b = lax.axis_index("blk")
    core = lax.rem(g, 2)
    rows, cols = part.shape
    half = rows // 2
    nz = n_grp // 2
    z = g // 2
    size = half // nz
    partner = g + 1 - 2 * core

    barrier = pltpu.get_barrier_semaphore()
    zpeers = [(lax.rem(g + 2 * k, n_grp), b) for k in range(1, nz)]
    bpeers = [(g, lax.rem(b + n_blk - k, n_blk)) for k in range(1, n_blk)]
    outer = (partner, lax.rem(b + n_blk - 1 + 2 * core, n_blk))
    out_does = jnp.where(core == 0, b > 0, b < n_blk - 1)
    for device in zpeers + bpeers + [(partner, b), outer]:
        pl.semaphore_signal(barrier, inc=1, device_id=device, device_id_type=MESH)
    pl.semaphore_wait(barrier, nz - 1 + n_blk - 1 + 2)

    give = pl.multiple_of((1 - core) * half, 8)
    keep = pl.multiple_of(core * half, 8)
    first = remote(part.at[pl.ds(give, half)], pair, sem_s.at[0], sem_r.at[0], (partner, b))
    first.start()
    back = [
        remote(drafts.at[k], dback.at[k - 1], dsem_s.at[k - 1], dsem_r.at[k - 1], bpeers[k - 1])
        for k in range(1, n_blk)
    ]
    for copy in back:
        copy.start()
    first.wait_recv()
    near[...] = part[pl.ds(keep, half), :] + pair[...]

    scatter = []
    for k in range(1, nz):
        to = lax.rem(z + k, nz)
        copy = remote(near.at[pl.ds(pl.multiple_of(to * size, 8), size)], far.at[k - 1],
                      sem_s.at[k], sem_r.at[k], zpeers[k - 1])
        copy.start()
        scatter.append(copy)
    mine = pl.multiple_of(z * size, 8)
    total = near[pl.ds(mine, size), :] + drive[pl.ds(pl.multiple_of(core * half + z * size, 8), size), :]
    for k in range(1, nz):
        scatter[k - 1].wait_recv()
        total = total + far[k - 1]
    source[pl.ds(pl.multiple_of(half + z * size, 8), size), :] = total

    spread = []
    for k in range(1, nz):
        block = source.at[pl.ds(pl.multiple_of(half + z * size, 8), size)]
        copy = remote(block, block, sem_s.at[nz + k], sem_r.at[nz + k], zpeers[k - 1])
        copy.start()
        spread.append(copy)
    for copy in spread:
        copy.wait_recv()

    middle = source.at[pl.ds(half, half)]
    there = pl.multiple_of(core * 2 * half, 8)
    away = pl.multiple_of((1 - core) * 2 * half, 8)
    swap = remote(middle, source.at[pl.ds(there, half)], sem_s.at[2 * nz], sem_r.at[2 * nz],
                  (partner, b))
    edge = remote(middle, source.at[pl.ds(away, half)], sem_s.at[2 * nz + 1],
                  sem_r.at[2 * nz + 1], outer)
    swap.start()

    @pl.when(out_does)
    def _():
        edge.start()

    @pl.when(jnp.logical_not(out_does))
    def _():
        source[pl.ds(there, half), :] = jnp.zeros((half, cols), F32)

    total = drafts[0]
    for k in range(1, n_blk):
        back[k - 1].wait_recv()
        total = total + dback[k - 1]
    draft_out[...] = total

    first.wait_send()
    for copy in back + scatter + spread:
        copy.wait_send()
    swap.wait()

    @pl.when(out_does)
    def _():
        edge.wait()


def swap_kernel(block, out, sem_s, sem_r):
    g = lax.axis_index("grp")
    b = lax.axis_index("blk")
    core = lax.rem(g, 2)
    partner = (g + 1 - 2 * core, b)
    half = block.shape[0]
    barrier = pltpu.get_barrier_semaphore()
    pl.semaphore_signal(barrier, inc=1, device_id=partner, device_id_type=MESH)
    pl.semaphore_wait(barrier, 1)
    here = pl.multiple_of(core * half, 8)
    copy = remote(block, out.at[pl.ds(here, half)], sem_s, sem_r, partner)
    copy.start()
    out[pl.ds(here, half), :] = block[...]
    copy.wait()


def ocean_kernel(n_grp, n_blk, temp, uvel, vvel, row_edge, col_edge, col, cav, top, draft, out):
    g = lax.axis_index("grp")
    b = lax.axis_index("blk")
    levels, rows, cols = temp.shape
    count = col.shape[1]
    melt = cav[...].astype(F32) * melt_rate * (top[...] + 0.5 + 0.5 * draft[...])
    ids = col[...]
    row = ids // cols
    lane = ids - row * cols
    hit = iota((rows, count), 0) == row
    pick = (iota((cols, count), 0) == lane).astype(F32).astype(BF16)
    high, low = split(melt)
    surface = nt(jnp.where(hit, high, 0.0).astype(BF16), pick)
    surface = surface + nt(jnp.where(hit, low, 0.0).astype(BF16), pick)

    west_in = (g > 0).astype(F32)
    east_in = (g < n_grp - 1).astype(F32)
    south_in = (b > 0).astype(F32)
    north_in = (b < n_blk - 1).astype(F32)
    at_row = iota((rows, cols), 0)
    at_col = iota((rows, cols), 1)

    def four(x, which, rowwise, colwise, k):
        found = []
        if rowwise:
            low = row_edge[0, which, k:k + 1, :] * west_in
            high = row_edge[1, which, k:k + 1, :] * east_in
            found.append(jnp.where(at_row == rows - 1, high, pltpu.roll(x, rows - 1, 0)))
            found.append(jnp.where(at_row == 0, low, pltpu.roll(x, 1, 0)))
        if colwise:
            low = col_edge[0, which, k] * south_in
            high = col_edge[1, which, k] * north_in
            found.append(jnp.where(at_col == cols - 1, high, pltpu.roll(x, cols - 1, 1)))
            found.append(jnp.where(at_col == 0, low, pltpu.roll(x, 1, 1)))
        return found

    for k in range(levels):
        t = temp[k]
        u = uvel[k]
        v = vvel[k]
        te, tw, tn, ts = four(t, 0, True, True, k)
        ue, uw = four(u, 1, True, False, k)
        vn, vs = four(v, 1, False, True, k)
        ue = 0.5 * (u + ue)
        uw = 0.5 * (u + uw)
        vn = 0.5 * (v + vn)
        vs = 0.5 * (v + vs)
        flux_east = jnp.maximum(ue, 0.0) * t + jnp.minimum(ue, 0.0) * te
        flux_west = jnp.maximum(uw, 0.0) * tw + jnp.minimum(uw, 0.0) * t
        flux_north = jnp.maximum(vn, 0.0) * t + jnp.minimum(vn, 0.0) * tn
        flux_south = jnp.maximum(vs, 0.0) * ts + jnp.minimum(vs, 0.0) * t
        laplace = te + tw + tn + ts - 4.0 * t
        vert = jnp.zeros_like(t)
        if k + 1 < levels:
            vert = vert + (temp[k + 1] - t)
        if k > 0:
            vert = vert - (t - temp[k - 1])
        new = (t + flux_west - flux_east + flux_south - flux_north + kappa * laplace
               + vertical_mix * vert)
        if k == 0:
            new = new - melt_rate * surface
        out[k] = new


def shift_rows(before, now, after):
    rows = now.shape[0]
    at = iota(now.shape, 0)
    above = jnp.where(at == 0, pltpu.roll(before, 1, 0), pltpu.roll(now, 1, 0))
    below = jnp.where(at == rows - 1, pltpu.roll(after, rows - 1, 0), pltpu.roll(now, rows - 1, 0))
    return above, below


def solve_kernel(n_blk, source, visc, fric, out, *scratch):
    g = lax.axis_index("grp")
    b = lax.axis_index("blk")
    core = lax.rem(g, 2)
    ext, wide = source.shape
    step = 8
    sizes = [(ext >> d, wide >> d) for d in range(LEVELS)]
    names = ("visc", "fric", "f", "a", "b", "e", "w", "n", "s", "d", "i")
    lev = [dict(zip(names, scratch[d * len(names):(d + 1) * len(names)])) for d in range(LEVELS)]
    down, right, up, left = scratch[LEVELS * len(names):]

    r, c = down.shape
    down[...] = jnp.where(iota((r, c), 1) // 2 == iota((r, c), 0), 0.25, 0.0).astype(BF16)
    r, c = up.shape
    up[...] = jnp.where(iota((r, c), 0) // 2 == iota((r, c), 1), 1.0, 0.0).astype(BF16)
    r, c = right.shape
    right[...] = jnp.where(iota((r, c), 0) // 2 == iota((r, c), 1), 1.0, 0.0).astype(BF16)
    r, c = left.shape
    left[...] = jnp.where(iota((r, c), 1) // 2 == iota((r, c), 0), 1.0, 0.0).astype(BF16)

    def restrict(x):
        r, c = x.shape
        paired = dot2(x, down[:r // 2, :r], left=True)
        return dot2(paired, right[:c, :c // 2])

    def prolong(x):
        r, c = x.shape
        tall = dot2(x, up[:2 * r, :r], left=True)
        return dot2(tall, left[:c, :2 * c])

    def chunks(d, body):
        rows = sizes[d][0]

        def run(index, carry):
            body(pl.multiple_of(index * step, step))
            return carry

        lax.fori_loop(0, rows // step, run, 0, unroll=2)

    def neighbours(ref, at):
        now = ref[pl.ds(at + step, step), :]
        before = ref[pl.ds(at, step), :]
        after = ref[pl.ds(at + 2 * step, step), :]
        above, below = shift_rows(before, now, after)
        cols = now.shape[1]
        return now, above, below, pltpu.roll(now, 1, 1), pltpu.roll(now, cols - 1, 1)

    for d in range(LEVELS):
        m = lev[d]
        rows, cols = sizes[d]
        zero = jnp.zeros((step, cols), F32)
        for name in ("visc", "a", "b"):
            m[name][0:step, :] = zero
            m[name][rows + step:rows + 2 * step, :] = zero
        m["visc"][step:rows + step, :] = visc[...] if d == 0 else restrict(
            lev[d - 1]["visc"][step:2 * rows + step, :])
        if d == 0:
            m["fric"][...] = fric[...]
        else:
            m["fric"][...] = restrict(lev[d - 1]["fric"][...])
        halo = ext // 3 >> d
        low = jnp.where(jnp.logical_and(core == 0, b == 0), halo, 0)
        high = jnp.where(jnp.logical_and(core == 1, b == n_blk - 1), rows - halo, rows)
        scale = 0.5 * 0.25 ** d

        def faces(at, m=m, cols=cols, low=low, high=high, scale=scale):
            now, above, below, west, east = neighbours(m["visc"], at)
            col = iota(now.shape, 1)
            fe = scale * (now + below)
            fw = scale * (now + above)
            fn = scale * (now + jnp.where(col == cols - 1, 0.0, east))
            fs = scale * (now + jnp.where(col == 0, 0.0, west))
            here = pl.ds(at, step)
            diag = fe + fw + fn + fs + m["fric"][here, :]
            row = iota(now.shape, 0) + at
            inside = jnp.logical_and(row >= low, row < high)
            m["d"][here, :] = diag
            m["i"][here, :] = jnp.where(inside, omega / diag, 0.0)
            m["e"][here, :] = fe
            m["w"][here, :] = fw
            m["n"][here, :] = jnp.where(col == cols - 1, 0.0, fn)
            m["s"][here, :] = jnp.where(col == 0, 0.0, fs)

        chunks(d, faces)

    def flux(m, ref, at):
        now, above, below, west, east = neighbours(ref, at)
        here = pl.ds(at, step)
        total = (m["f"][here, :] + m["e"][here, :] * below + m["w"][here, :] * above
                 + m["n"][here, :] * east + m["s"][here, :] * west)
        return now, total

    def sweep(d, old, new):
        m = lev[d]

        def body(at):
            now, total = flux(m, m[old], at)
            m[new][pl.ds(at + step, step), :] = (1.0 - omega) * now + m["i"][pl.ds(at, step), :] * total

        chunks(d, body)

    def first(d, new):
        m = lev[d]

        def body(at):
            here = pl.ds(at, step)
            m[new][pl.ds(at + step, step), :] = m["i"][here, :] * m["f"][here, :]

        chunks(d, body)

    def residual(d, old, new):
        m = lev[d]

        def body(at):
            now, total = flux(m, m[old], at)
            m[new][pl.ds(at + step, step), :] = total - m["d"][pl.ds(at, step), :] * now

        chunks(d, body)

    def vcycle(d, zero):
        m = lev[d]
        rows, cols = sizes[d]
        sweeps = COARSE_SWEEPS if d == LEVELS - 1 else SMOOTH_SWEEPS
        names = ("a", "b") if sweeps % 2 == 0 else ("b", "a")
        for index in range(sweeps):
            old, new = ("a", "b") if index % 2 == 0 else ("b", "a")
            if index == 0 and zero:
                first(d, new)
            else:
                sweep(d, old, new)
        if d == LEVELS - 1:
            return
        residual(d, "a", "b")
        lev[d + 1]["f"][...] = restrict(m["b"][step:rows + step, :])
        vcycle(d + 1, True)
        m["a"][step:rows + step, :] += prolong(lev[d + 1]["a"][step:rows // 2 + step, :])
        for index in range(SMOOTH_SWEEPS):
            old, new = ("a", "b") if index % 2 == 0 else ("b", "a")
            sweep(d, old, new)

    lev[0]["f"][...] = source[...]
    for cycle_index in range(CYCLES):
        vcycle(0, cycle_index == 0)
    third = ext // 3
    out[...] = lev[0]["a"][third + step:2 * third + step, :]


def params(collective=None):
    if collective is None:
        return pltpu.CompilerParams(vmem_limit_bytes=LIMIT)
    return pltpu.CompilerParams(
        vmem_limit_bytes=LIMIT, collective_id=collective, has_side_effects=True)


def shards(n_grp, n_blk, temp, uvel, vvel, couple_col, couple_cell, cavity, thickness, viscosity,
           friction, drive):
    levels, orows, ocols = temp.shape
    rows, cols = thickness.shape
    half = rows // 2
    count = couple_col.shape[-1]
    col = couple_col.reshape(1, count)
    cell = couple_cell.reshape(1, count)
    cav = cavity.reshape(1, count)
    row_edge = jnp.stack([jnp.stack([temp[:, 0, :], uvel[:, 0, :]]),
                          jnp.stack([temp[:, -1, :], uvel[:, -1, :]])])
    col_edge = jnp.stack([jnp.stack([temp[:, :, 0], vvel[:, :, 0]]),
                          jnp.stack([temp[:, :, -1], vvel[:, :, -1]])])

    def shape(*dims):
        return jax.ShapeDtypeStruct(dims, F32)

    part, drafts, top, visc, fric, row_in, col_in = pl.pallas_call(
        functools.partial(couple_kernel, n_grp, n_blk),
        out_shape=(shape(rows, cols), shape(n_blk, 1, count), shape(1, count),
                   shape(3 * half, cols), shape(3 * half, cols),
                   shape(2, 2, levels, ocols), shape(2, 2, levels, orows)),
        in_specs=[VM] * 9,
        out_specs=(VM,) * 7,
        scratch_shapes=[
            pltpu.VMEM((n_blk - 1, 1, count), jnp.int32),
            pltpu.VMEM((n_blk - 1, 1, count), jnp.int32),
            pltpu.VMEM((n_blk, 1, count), F32),
            pltpu.VMEM((3 * rows, cols), F32),
            pltpu.SemaphoreType.DMA((n_blk - 1, 3)),
            pltpu.SemaphoreType.DMA((n_blk - 1, 3)),
            pltpu.SemaphoreType.DMA((6,)),
            pltpu.SemaphoreType.DMA((6,)),
        ],
        compiler_params=params(0),
        name="couple",
    )(temp[0], col, cell, cav, thickness, viscosity, friction, row_edge, col_edge)

    nz = n_grp // 2
    source, draft = pl.pallas_call(
        functools.partial(reduce_kernel, n_grp, n_blk),
        out_shape=(shape(3 * half, cols), shape(1, count)),
        in_specs=[VM] * 3,
        out_specs=(VM,) * 2,
        scratch_shapes=[
            pltpu.VMEM((half, cols), F32),
            pltpu.VMEM((half, cols), F32),
            pltpu.VMEM((nz - 1, half // nz, cols), F32),
            pltpu.VMEM((n_blk - 1, 1, count), F32),
            pltpu.SemaphoreType.DMA((2 * nz + 2,)),
            pltpu.SemaphoreType.DMA((2 * nz + 2,)),
            pltpu.SemaphoreType.DMA((n_blk - 1,)),
            pltpu.SemaphoreType.DMA((n_blk - 1,)),
        ],
        compiler_params=params(1),
        name="reduce",
    )(part, drive, drafts)

    ext = 3 * half
    scratch = []
    for depth in range(LEVELS):
        r, c = ext >> depth, cols >> depth
        tall, flat = pltpu.VMEM((r + 16, c), F32), pltpu.VMEM((r, c), F32)
        scratch += [tall, flat, flat, tall, tall] + [flat] * 6
    scratch += [pltpu.VMEM((ext // 2, ext), BF16), pltpu.VMEM((cols, cols // 2), BF16),
                pltpu.VMEM((ext, ext // 2), BF16), pltpu.VMEM((cols // 2, cols), BF16)]
    block = pl.pallas_call(
        functools.partial(solve_kernel, n_blk),
        out_shape=shape(half, cols),
        in_specs=[VM] * 3,
        out_specs=VM,
        scratch_shapes=scratch,
        compiler_params=params(),
        name="solve",
    )(source, visc, fric)

    velocity = pl.pallas_call(
        swap_kernel,
        out_shape=shape(rows, cols),
        in_specs=[VM],
        out_specs=VM,
        scratch_shapes=[pltpu.SemaphoreType.DMA, pltpu.SemaphoreType.DMA],
        compiler_params=params(2),
        name="swap",
    )(block)

    temp_new = pl.pallas_call(
        functools.partial(ocean_kernel, n_grp, n_blk),
        out_shape=shape(levels, orows, ocols),
        in_specs=[VM] * 9,
        out_specs=VM,
        compiler_params=params(),
        name="ocean",
    )(temp, uvel, vvel, row_in, col_in[..., None], col, cav, top, draft)
    return (temp_new, velocity)


def solution(mesh):
    sizes = dict(mesh.shape)
    return jax.shard_map(
        functools.partial(shards, sizes["grp"], sizes["blk"]),
        mesh=mesh,
        in_specs=(
            P(None, "grp", "blk"),
            P(None, "grp", "blk"),
            P(None, "grp", "blk"),
            P("grp", "blk", None),
            P("grp", "blk", None),
            P("grp", "blk", None),
            P("blk", None),
            P("blk", None),
            P("blk", None),
            P("blk", None),
        ),
        out_specs=(P(None, "grp", "blk"), P("blk", None)),
        check_vma=False,
    )
```

```python
import functools

import jax
import jax.numpy as jnp
from jax import lax
from jax.experimental import pallas as pl
from jax.experimental.pallas import tpu as pltpu
from jax.sharding import PartitionSpec as P

LEVELS = 3
SMOOTH_SWEEPS = 2
COARSE_SWEEPS = 4
CYCLES = 2

omega = 0.8
kappa = 0.1
vertical_mix = 0.2
melt_rate = 0.5

MESH = pl.DeviceIdType.MESH
VM = pl.BlockSpec(memory_space=pltpu.VMEM)
LIMIT = 56 * 1024 * 1024
F32 = jnp.float32
BF16 = jnp.bfloat16


def split(x):
    high = x.astype(BF16).astype(F32)
    return high, x - high


def dot2(x, one, left=False):
    out = None
    for part in split(x):
        part = part.astype(BF16)
        term = jnp.dot(one, part, preferred_element_type=F32) if left else jnp.dot(
            part, one, preferred_element_type=F32)
        out = term if out is None else out + term
    return out


def nt(a, b):
    return lax.dot_general(a, b, (((1,), (1,)), ((), ())), preferred_element_type=F32)


def iota(shape, dim):
    return lax.broadcasted_iota(jnp.int32, shape, dim)


def remote(src, dst, send, recv, device):
    return pltpu.make_async_remote_copy(
        src_ref=src, dst_ref=dst, send_sem=send, recv_sem=recv, device_id=device,
        device_id_type=MESH)


def ocean(n_grp, n_blk, g, b, temp, uvel, vvel, row_edge, col_edge, col, melt, out):
    levels, rows, cols = temp.shape
    count = col.shape[1]
    ids = col[...]
    row = ids // cols
    lane = ids - row * cols
    hit = iota((rows, count), 0) == row
    pick = (iota((cols, count), 0) == lane).astype(F32).astype(BF16)
    high, low = split(melt)
    surface = nt(jnp.where(hit, high, 0.0).astype(BF16), pick)
    surface = surface + nt(jnp.where(hit, low, 0.0).astype(BF16), pick)

    west_in = (g > 0).astype(F32)
    east_in = (g < n_grp - 1).astype(F32)
    south_in = (b > 0).astype(F32)
    north_in = (b < n_blk - 1).astype(F32)
    at_row = iota((rows, cols), 0)
    at_col = iota((rows, cols), 1)

    def four(x, which, rowwise, colwise, k):
        found = []
        if rowwise:
            low = row_edge[0, which, k:k + 1, :] * west_in
            high = row_edge[1, which, k:k + 1, :] * east_in
            found.append(jnp.where(at_row == rows - 1, high, pltpu.roll(x, rows - 1, 0)))
            found.append(jnp.where(at_row == 0, low, pltpu.roll(x, 1, 0)))
        if colwise:
            lane = which * levels + k
            low = col_edge[0, :, lane:lane + 1] * south_in
            high = col_edge[1, :, lane:lane + 1] * north_in
            found.append(jnp.where(at_col == cols - 1, high, pltpu.roll(x, cols - 1, 1)))
            found.append(jnp.where(at_col == 0, low, pltpu.roll(x, 1, 1)))
        return found

    for k in range(levels):
        t = temp[k]
        u = uvel[k]
        v = vvel[k]
        te, tw, tn, ts = four(t, 0, True, True, k)
        ue, uw = four(u, 1, True, False, k)
        vn, vs = four(v, 1, False, True, k)
        ue = 0.5 * (u + ue)
        uw = 0.5 * (u + uw)
        vn = 0.5 * (v + vn)
        vs = 0.5 * (v + vs)
        flux_east = jnp.maximum(ue, 0.0) * t + jnp.minimum(ue, 0.0) * te
        flux_west = jnp.maximum(uw, 0.0) * tw + jnp.minimum(uw, 0.0) * t
        flux_north = jnp.maximum(vn, 0.0) * t + jnp.minimum(vn, 0.0) * tn
        flux_south = jnp.maximum(vs, 0.0) * ts + jnp.minimum(vs, 0.0) * t
        laplace = te + tw + tn + ts - 4.0 * t
        vert = jnp.zeros_like(t)
        if k + 1 < levels:
            vert = vert + (temp[k + 1] - t)
        if k > 0:
            vert = vert - (t - temp[k - 1])
        new = (t + flux_west - flux_east + flux_south - flux_north + kappa * laplace
               + vertical_mix * vert)
        if k == 0:
            new = new - melt_rate * surface
        out[k] = new


def shift_rows(before, now, after):
    rows = now.shape[0]
    at = iota(now.shape, 0)
    above = jnp.where(at == 0, pltpu.roll(before, 1, 0), pltpu.roll(now, 1, 0))
    below = jnp.where(at == rows - 1, pltpu.roll(after, rows - 1, 0), pltpu.roll(now, rows - 1, 0))
    return above, below


def multigrid(n_blk, core, b, scratch):
    step = 8
    ext, wide = scratch[1].shape
    sizes = [(ext >> d, wide >> d) for d in range(LEVELS)]
    names = ("visc", "fric", "f", "a", "b", "e", "w", "n", "s", "d", "i")
    lev = [dict(zip(names, scratch[d * len(names):(d + 1) * len(names)])) for d in range(LEVELS)]
    down, right, up, left = scratch[LEVELS * len(names):]

    def matrices():
        r, c = down.shape
        down[...] = jnp.where(iota((r, c), 1) // 2 == iota((r, c), 0), 0.25, 0.0).astype(BF16)
        r, c = up.shape
        up[...] = jnp.where(iota((r, c), 0) // 2 == iota((r, c), 1), 1.0, 0.0).astype(BF16)
        r, c = right.shape
        right[...] = jnp.where(iota((r, c), 0) // 2 == iota((r, c), 1), 1.0, 0.0).astype(BF16)
        r, c = left.shape
        left[...] = jnp.where(iota((r, c), 1) // 2 == iota((r, c), 0), 1.0, 0.0).astype(BF16)

    def restrict(x):
        r, c = x.shape
        paired = dot2(x, down[:r // 2, :r], left=True)
        return dot2(paired, right[:c, :c // 2])

    def prolong(x):
        r, c = x.shape
        tall = dot2(x, up[:2 * r, :r], left=True)
        return dot2(tall, left[:c, :2 * c])

    def chunks(d, body, trim=0):
        rows = sizes[d][0]
        low = (trim >> d) // step
        count = rows // step - 2 * low

        def run(index, carry):
            body(pl.multiple_of((index + low) * step, step))
            return carry

        lax.fori_loop(0, count, run, 0, unroll=4 if count % 4 == 0 else 2)

    def neighbours(ref, at):
        now = ref[pl.ds(at + step, step), :]
        before = ref[pl.ds(at, step), :]
        after = ref[pl.ds(at + 2 * step, step), :]
        above, below = shift_rows(before, now, after)
        cols = now.shape[1]
        return now, above, below, pltpu.roll(now, 1, 1), pltpu.roll(now, cols - 1, 1)

    def coefficients():
        for d in range(LEVELS):
            m = lev[d]
            rows, cols = sizes[d]
            zero = jnp.zeros((step, cols), F32)
            for name in ("visc", "a", "b"):
                m[name][0:step, :] = zero
                m[name][rows + step:rows + 2 * step, :] = zero
            if d > 0:
                m["visc"][step:rows + step, :] = restrict(lev[d - 1]["visc"][step:2 * rows + step, :])
                m["fric"][...] = restrict(lev[d - 1]["fric"][...])
            halo = ext // 3 >> d
            low = jnp.where(jnp.logical_and(core == 0, b == 0), halo, 0)
            high = jnp.where(jnp.logical_and(core == 1, b == n_blk - 1), rows - halo, rows)
            scale = 0.5 * 0.25 ** d

            def faces(at, m=m, cols=cols, low=low, high=high, scale=scale):
                now, above, below, west, east = neighbours(m["visc"], at)
                col = iota(now.shape, 1)
                fe = scale * (now + below)
                fw = scale * (now + above)
                fn = scale * (now + jnp.where(col == cols - 1, 0.0, east))
                fs = scale * (now + jnp.where(col == 0, 0.0, west))
                here = pl.ds(at, step)
                diag = fe + fw + fn + fs + m["fric"][here, :]
                row = iota(now.shape, 0) + at
                inside = jnp.logical_and(row >= low, row < high)
                m["d"][here, :] = diag
                m["i"][here, :] = jnp.where(inside, omega / diag, 0.0)
                m["e"][here, :] = fe
                m["w"][here, :] = fw
                m["n"][here, :] = jnp.where(col == cols - 1, 0.0, fn)
                m["s"][here, :] = jnp.where(col == 0, 0.0, fs)

            chunks(d, faces)

    def flux(m, ref, at):
        now, above, below, west, east = neighbours(ref, at)
        here = pl.ds(at, step)
        total = (m["f"][here, :] + m["e"][here, :] * below + m["w"][here, :] * above
                 + m["n"][here, :] * east + m["s"][here, :] * west)
        return now, total

    def sweep(d, old, new, trim):
        m = lev[d]

        def body(at):
            now, total = flux(m, m[old], at)
            m[new][pl.ds(at + step, step), :] = (1.0 - omega) * now + m["i"][pl.ds(at, step), :] * total

        chunks(d, body, trim)

    def first(d, new, trim):
        m = lev[d]

        def body(at):
            here = pl.ds(at, step)
            m[new][pl.ds(at + step, step), :] = m["i"][here, :] * m["f"][here, :]

        chunks(d, body, trim)

    def residual(d, old, new, trim):
        m = lev[d]

        def body(at):
            now, total = flux(m, m[old], at)
            m[new][pl.ds(at + step, step), :] = total - m["d"][pl.ds(at, step), :] * now

        chunks(d, body, trim)

    def vcycle(d, zero, trim, after):
        m = lev[d]
        rows, cols = sizes[d]
        sweeps = COARSE_SWEEPS if d == LEVELS - 1 else SMOOTH_SWEEPS
        for index in range(sweeps):
            old, new = ("a", "b") if index % 2 == 0 else ("b", "a")
            if index == 0 and zero:
                first(d, new, trim)
            else:
                sweep(d, old, new, trim)
        if d == LEVELS - 1:
            return
        residual(d, "a", "b", trim)
        low, high = trim >> d, rows - (trim >> d)
        lev[d + 1]["f"][low // 2:high // 2, :] = restrict(m["b"][low + step:high + step, :])
        vcycle(d + 1, True, trim, trim)
        m["a"][low + step:high + step, :] += prolong(
            lev[d + 1]["a"][low // 2 + step:high // 2 + step, :])
        for index in range(SMOOTH_SWEEPS):
            old, new = ("a", "b") if index % 2 == 0 else ("b", "a")
            sweep(d, old, new, after)

    def cycles():
        inner = ext // 6
        for cycle_index in range(CYCLES):
            vcycle(0, cycle_index == 0, 0 if cycle_index < CYCLES - 1 else inner, inner)

    return lev[0], matrices, coefficients, cycles


def step_kernel(n_grp, n_blk, temp, uvel, vvel, col, cell, cav, thick, visc, fric, drive,
                temp_out, vel_out, ent_cell, ent_cav, ent_w, acc, drafts, dback, row_edge,
                col_edge, row_in, col_in, part, near, pair, far, esem_s, esem_r, hsem_s, hsem_r,
                bsem_s, bsem_r, zsem_s, zsem_r, gsem_s, gsem_r, psem_s, psem_r, osem_s, osem_r,
                sem_s, sem_r, *scratch):
    g = lax.axis_index("grp")
    b = lax.axis_index("blk")
    core = lax.rem(g, 2)
    z = g // 2
    nz = n_grp // 2
    rows, cols = thick.shape
    half = rows // 2
    size = half // nz
    count = cell.shape[1]
    levels, ocean_rows, ocean_cols = temp.shape
    up_g, dn_g = lax.rem(g + 1, n_grp), lax.rem(g + n_grp - 1, n_grp)
    up_b, dn_b = lax.rem(b + 1, n_blk), lax.rem(b + n_blk - 1, n_blk)
    partner = g + 1 - 2 * core
    outer = (partner, lax.rem(b + n_blk - 1 + 2 * core, n_blk))
    fine, matrices, coefficients, cycles = multigrid(n_blk, core, b, scratch)
    pad = 8

    def aligned(x):
        return pl.multiple_of(x, 8)

    barrier = pltpu.get_barrier_semaphore()
    peers = [(g, lax.rem(b + k, n_blk)) for k in range(1, n_blk)]
    bpeers = [(g, lax.rem(b + n_blk - k, n_blk)) for k in range(1, n_blk)]
    zpeers = [(lax.rem(g + 2 * k, n_grp), b) for k in range(1, nz)]
    greet = peers + [(up_g, b), (dn_g, b), (partner, b), outer] + zpeers
    for device in greet:
        pl.semaphore_signal(barrier, inc=1, device_id=device, device_id_type=MESH)
    at_lane = iota((ocean_rows, ocean_cols), 1)
    for side in range(2):
        edge = jnp.zeros((ocean_rows, ocean_cols), F32)
        r, c = (0, 0) if side == 0 else (ocean_rows - 1, ocean_cols - 1)
        for k in range(levels):
            row_edge[side, 0, k:k + 1, :] = temp[k, r:r + 1, :]
            row_edge[side, 1, k:k + 1, :] = uvel[k, r:r + 1, :]
            for which, ref in enumerate((temp, vvel)):
                lane = which * levels + k
                moved = pltpu.roll(ref[k], (lane - c) % ocean_cols, 1)
                edge = jnp.where(at_lane == lane, moved, edge)
        col_edge[side] = edge
    pl.semaphore_wait(barrier, len(greet))

    ent = []
    for k in range(1, n_blk):
        target = peers[k - 1]
        trio = [
            remote(cell, ent_cell.at[k - 1], esem_s.at[k - 1, 0], esem_r.at[k - 1, 0], target),
            remote(cav, ent_cav.at[k - 1], esem_s.at[k - 1, 1], esem_r.at[k - 1, 1], target),
            remote(ent_w.at[0], ent_w.at[k], esem_s.at[k - 1, 2], esem_r.at[k - 1, 2], target),
        ]
        trio[0].start()
        trio[1].start()
        ent.append(trio)

    ids = col[...]
    ocean_row = ids // ocean_cols
    ocean_lane = ids - ocean_row * ocean_cols
    pick = (iota((ocean_cols, count), 0) == ocean_lane).astype(F32).astype(BF16)
    surface = temp[0]
    rest = split(split(surface)[1])[1]
    wide = dot2(surface, pick) + jnp.dot(rest.astype(BF16), pick, preferred_element_type=F32)
    top = jnp.sum(jnp.where(iota((ocean_rows, count), 0) == ocean_row, wide, 0.0), axis=0,
                  keepdims=True)
    ent_w[0] = cav[...].astype(F32) * melt_rate * (top + 0.5)
    for trio in ent:
        trio[2].start()

    edges = [
        remote(row_edge.at[1], row_in.at[0], hsem_s.at[0], hsem_r.at[0], (up_g, b)),
        remote(row_edge.at[0], row_in.at[1], hsem_s.at[1], hsem_r.at[1], (dn_g, b)),
        remote(col_edge.at[1], col_in.at[0], hsem_s.at[2], hsem_r.at[2], (g, up_b)),
        remote(col_edge.at[0], col_in.at[1], hsem_s.at[3], hsem_r.at[3], (g, dn_b)),
    ]
    for copy in edges:
        copy.start()
    own = aligned((1 - core) * half)
    halo = aligned(core * 2 * half)
    target = (g, lax.rem(b + n_blk + 1 - 2 * core, n_blk))
    does = jnp.where(core == 0, b < n_blk - 1, b > 0)
    gets = jnp.where(core == 0, b > 0, b < n_blk - 1)
    ice = [
        remote(visc.at[pl.ds(own, half)], fine["visc"].at[pl.ds(halo + pad, half)], hsem_s.at[4],
               hsem_r.at[4], target),
        remote(fric.at[pl.ds(own, half)], fine["fric"].at[pl.ds(halo, half)], hsem_s.at[5],
               hsem_r.at[5], target),
    ]

    @pl.when(does)
    def _():
        for copy in ice:
            copy.start()

    fine["visc"][pl.ds(own + pad, 2 * half), :] = visc[...]
    fine["fric"][pl.ds(own, 2 * half), :] = fric[...]

    @pl.when(jnp.logical_not(gets))
    def _():
        fine["visc"][pl.ds(halo + pad, half), :] = jnp.zeros((half, cols), F32)
        fine["fric"][pl.ds(halo, half), :] = jnp.ones((half, cols), F32)

    high, low = split(thick[...])
    thick2 = jnp.concatenate([high, low], axis=0).astype(BF16)
    acc[...] = jnp.zeros_like(acc)
    chunk = min(512, count)
    for k in range(n_blk):
        if k > 0:
            for copy in ent[k - 1]:
                copy.wait_recv()
        cells_ref = cell if k == 0 else ent_cell.at[k - 1]
        cav_ref = cav if k == 0 else ent_cav.at[k - 1]

        for piece in range(count // chunk):
            at = slice(piece * chunk, (piece + 1) * chunk)
            cells = cells_ref[:, at]
            grid_row = cells // cols
            lane = cells - grid_row * cols
            hit = iota((rows, chunk), 0) == grid_row - b * rows
            pick = (iota((cols, chunk), 0) == lane).astype(F32).astype(BF16)
            found = jnp.dot(thick2, pick, preferred_element_type=F32)
            draft = jnp.sum(jnp.where(hit, found[:rows] + found[rows:], 0.0), axis=0, keepdims=True)
            drafts[k, :, at] = draft
            melt = ent_w[k, :, at] + cav_ref[:, at].astype(F32) * (0.5 * melt_rate) * draft
            m_high, m_low = split(melt)
            spread = jnp.concatenate(
                [jnp.where(hit, m_high, 0.0).astype(BF16), jnp.where(hit, m_low, 0.0).astype(BF16)],
                axis=0)
            acc[...] += nt(spread, pick)

    part[...] = acc[:rows] + acc[rows:]

    give = aligned((1 - core) * half)
    keep = aligned(core * half)
    first = remote(part.at[pl.ds(give, half)], pair, sem_s.at[0], sem_r.at[0], (partner, b))
    first.start()
    back = [
        remote(drafts.at[k], dback.at[k - 1], bsem_s.at[k - 1], bsem_r.at[k - 1], bpeers[k - 1])
        for k in range(1, n_blk)
    ]
    for copy in back:
        copy.start()
    matrices()
    first.wait_recv()
    near[...] = part[pl.ds(keep, half), :] + pair[...]

    scatter = []
    for k in range(1, nz):
        to = lax.rem(z + k, nz)
        copy = remote(near.at[pl.ds(aligned(to * size), size)], far.at[k - 1],
                      zsem_s.at[k - 1], zsem_r.at[k - 1], zpeers[k - 1])
        copy.start()
        scatter.append(copy)

    @pl.when(gets)
    def _():
        for copy in ice:
            copy.wait_recv()

    coefficients()

    source = fine["f"]
    mine = aligned(z * size)
    total = near[pl.ds(mine, size), :] + drive[pl.ds(aligned(core * half + z * size), size), :]
    for k in range(1, nz):
        scatter[k - 1].wait_recv()
        total = total + far[k - 1]
    source[pl.ds(aligned(half + z * size), size), :] = total

    there = core * 2 * half
    away = (1 - core) * 2 * half
    out_does = jnp.where(core == 0, b > 0, b < n_blk - 1)
    spread, swaps, outs = [], [], []
    for k in range(1, nz):
        block = source.at[pl.ds(aligned(half + z * size), size)]
        copy = remote(block, block, gsem_s.at[k - 1], gsem_r.at[k - 1], zpeers[k - 1])
        copy.start()
        spread.append(copy)

    def forward(k):
        at = lax.rem(z + nz - k, nz) * size
        block = source.at[pl.ds(aligned(half + at), size)]
        swap = remote(block, source.at[pl.ds(aligned(there + at), size)], psem_s.at[k],
                      psem_r.at[k], (partner, b))
        out = remote(block, source.at[pl.ds(aligned(away + at), size)], osem_s.at[k],
                     osem_r.at[k], outer)
        swap.start()
        swaps.append(swap)
        outs.append(out)

        @pl.when(out_does)
        def _():
            out.start()

    forward(0)

    @pl.when(jnp.logical_not(out_does))
    def _():
        source[pl.ds(aligned(there), half), :] = jnp.zeros((half, cols), F32)

    for copy in edges:
        copy.wait()
    draft = drafts[0]
    for k in range(1, n_blk):
        back[k - 1].wait_recv()
        draft = draft + dback[k - 1]
    for k in range(1, nz):
        spread[k - 1].wait_recv()
        forward(k)

    melt = ent_w[0] + cav[...].astype(F32) * (0.5 * melt_rate) * draft
    ocean(n_grp, n_blk, g, b, temp, uvel, vvel, row_in, col_in, col, melt, temp_out)

    for copy in swaps:
        copy.wait()

    @pl.when(out_does)
    def _():
        for copy in outs:
            copy.wait()

    cycles()

    here = aligned(core * half)
    block = fine["a"].at[pl.ds(half + pad, half)]
    last = remote(block, vel_out.at[pl.ds(here, half)], sem_s.at[1], sem_r.at[1], (partner, b))
    last.start()
    vel_out[pl.ds(here, half), :] = fine["a"][half + pad:2 * half + pad, :]
    for trio in ent:
        for copy in trio:
            copy.wait_send()

    @pl.when(does)
    def _():
        for copy in ice:
            copy.wait_send()

    first.wait_send()
    for copy in back + scatter + spread:
        copy.wait_send()
    last.wait()


def shards(n_grp, n_blk, temp, uvel, vvel, couple_col, couple_cell, cavity, thickness, viscosity,
           friction, drive):
    levels, orows, ocols = temp.shape
    rows, cols = thickness.shape
    half = rows // 2
    count = couple_col.shape[-1]
    nz = n_grp // 2
    ext = 3 * half
    scratch = []
    for depth in range(LEVELS):
        r, c = ext >> depth, cols >> depth
        tall, flat = pltpu.VMEM((r + 16, c), F32), pltpu.VMEM((r, c), F32)
        scratch += [tall, flat, flat, tall, tall] + [flat] * 6
    scratch += [pltpu.VMEM((ext // 2, ext), BF16), pltpu.VMEM((cols, cols // 2), BF16),
                pltpu.VMEM((ext, ext // 2), BF16), pltpu.VMEM((cols // 2, cols), BF16)]

    def pair_of(*dims):
        return [pltpu.SemaphoreType.DMA(dims)] * 2

    return pl.pallas_call(
        functools.partial(step_kernel, n_grp, n_blk),
        out_shape=(jax.ShapeDtypeStruct((levels, orows, ocols), F32),
                   jax.ShapeDtypeStruct((rows, cols), F32)),
        in_specs=[VM] * 10,
        out_specs=(VM,) * 2,
        scratch_shapes=[
            pltpu.VMEM((n_blk - 1, 1, count), jnp.int32),
            pltpu.VMEM((n_blk - 1, 1, count), jnp.int32),
            pltpu.VMEM((n_blk, 1, count), F32),
            pltpu.VMEM((2 * rows, cols), F32),
            pltpu.VMEM((n_blk, 1, count), F32),
            pltpu.VMEM((n_blk - 1, 1, count), F32),
            pltpu.VMEM((2, 2, levels, ocols), F32),
            pltpu.VMEM((2, orows, ocols), F32),
            pltpu.VMEM((2, 2, levels, ocols), F32),
            pltpu.VMEM((2, orows, ocols), F32),
            pltpu.VMEM((rows, cols), F32),
            pltpu.VMEM((half, cols), F32),
            pltpu.VMEM((half, cols), F32),
            pltpu.VMEM((nz - 1, half // nz, cols), F32),
        ] + pair_of(n_blk - 1, 3) + pair_of(6) + pair_of(n_blk - 1) + pair_of(nz - 1)
        + pair_of(nz - 1) + pair_of(nz) + pair_of(nz) + pair_of(2) + scratch,
        compiler_params=pltpu.CompilerParams(
            vmem_limit_bytes=LIMIT, collective_id=0, has_side_effects=True),
        name="step",
    )(temp, uvel, vvel, couple_col.reshape(1, count), couple_cell.reshape(1, count),
      cavity.reshape(1, count), thickness, viscosity, friction, drive)


def solution(mesh):
    sizes = dict(mesh.shape)
    return jax.shard_map(
        functools.partial(shards, sizes["grp"], sizes["blk"]),
        mesh=mesh,
        in_specs=(
            P(None, "grp", "blk"),
            P(None, "grp", "blk"),
            P(None, "grp", "blk"),
            P("grp", "blk", None),
            P("grp", "blk", None),
            P("grp", "blk", None),
            P("blk", None),
            P("blk", None),
            P("blk", None),
            P("blk", None),
        ),
        out_specs=(P(None, "grp", "blk"), P("blk", None)),
        check_vma=False,
    )
```

```python
import functools

import jax
import jax.numpy as jnp
from jax import lax
from jax.experimental import pallas as pl
from jax.experimental.pallas import tpu as pltpu
from jax.sharding import PartitionSpec as P

LEVELS = 3
SMOOTH_SWEEPS = 2
COARSE_SWEEPS = 4
CYCLES = 2

omega = 0.8
kappa = 0.1
vertical_mix = 0.2
melt_rate = 0.5

MESH = pl.DeviceIdType.MESH
VM = pl.BlockSpec(memory_space=pltpu.VMEM)
LIMIT = 56 * 1024 * 1024
F32 = jnp.float32
BF16 = jnp.bfloat16


def split(x):
    high = x.astype(BF16).astype(F32)
    return high, x - high


def dot2(x, one, left=False):
    out = None
    for part in split(x):
        part = part.astype(BF16)
        term = jnp.dot(one, part, preferred_element_type=F32) if left else jnp.dot(
            part, one, preferred_element_type=F32)
        out = term if out is None else out + term
    return out


def nt(a, b):
    return lax.dot_general(a, b, (((1,), (1,)), ((), ())), preferred_element_type=F32)


def iota(shape, dim):
    return lax.broadcasted_iota(jnp.int32, shape, dim)


def remote(src, dst, send, recv, device):
    return pltpu.make_async_remote_copy(
        src_ref=src, dst_ref=dst, send_sem=send, recv_sem=recv, device_id=device,
        device_id_type=MESH)


def ocean(n_grp, n_blk, g, b, temp, uvel, vvel, row_edge, col_edge, col, melt, out):
    levels, rows, cols = temp.shape
    count = col.shape[1]
    ids = col[...]
    row = ids // cols
    lane = ids - row * cols
    hit = iota((rows, count), 0) == row
    pick = (iota((cols, count), 0) == lane).astype(F32).astype(BF16)
    high, low = split(melt)
    surface = nt(jnp.where(hit, high, 0.0).astype(BF16), pick)
    surface = surface + nt(jnp.where(hit, low, 0.0).astype(BF16), pick)

    west_in = (g > 0).astype(F32)
    east_in = (g < n_grp - 1).astype(F32)
    south_in = (b > 0).astype(F32)
    north_in = (b < n_blk - 1).astype(F32)
    at_row = iota((rows, cols), 0)
    at_col = iota((rows, cols), 1)

    def four(x, which, rowwise, colwise, k):
        found = []
        if rowwise:
            low = row_edge[0, which, k:k + 1, :] * west_in
            high = row_edge[1, which, k:k + 1, :] * east_in
            found.append(jnp.where(at_row == rows - 1, high, pltpu.roll(x, rows - 1, 0)))
            found.append(jnp.where(at_row == 0, low, pltpu.roll(x, 1, 0)))
        if colwise:
            lane = which * levels + k
            low = col_edge[0, :, lane:lane + 1] * south_in
            high = col_edge[1, :, lane:lane + 1] * north_in
            found.append(jnp.where(at_col == cols - 1, high, pltpu.roll(x, cols - 1, 1)))
            found.append(jnp.where(at_col == 0, low, pltpu.roll(x, 1, 1)))
        return found

    for k in range(levels):
        t = temp[k]
        u = uvel[k]
        v = vvel[k]
        te, tw, tn, ts = four(t, 0, True, True, k)
        ue, uw = four(u, 1, True, False, k)
        vn, vs = four(v, 1, False, True, k)
        ue = 0.5 * (u + ue)
        uw = 0.5 * (u + uw)
        vn = 0.5 * (v + vn)
        vs = 0.5 * (v + vs)
        flux_east = jnp.maximum(ue, 0.0) * t + jnp.minimum(ue, 0.0) * te
        flux_west = jnp.maximum(uw, 0.0) * tw + jnp.minimum(uw, 0.0) * t
        flux_north = jnp.maximum(vn, 0.0) * t + jnp.minimum(vn, 0.0) * tn
        flux_south = jnp.maximum(vs, 0.0) * ts + jnp.minimum(vs, 0.0) * t
        laplace = te + tw + tn + ts - 4.0 * t
        vert = jnp.zeros_like(t)
        if k + 1 < levels:
            vert = vert + (temp[k + 1] - t)
        if k > 0:
            vert = vert - (t - temp[k - 1])
        new = (t + flux_west - flux_east + flux_south - flux_north + kappa * laplace
               + vertical_mix * vert)
        if k == 0:
            new = new - melt_rate * surface
        out[k] = new


def shift_rows(before, now, after):
    rows = now.shape[0]
    at = iota(now.shape, 0)
    above = jnp.where(at == 0, pltpu.roll(before, 1, 0), pltpu.roll(now, 1, 0))
    below = jnp.where(at == rows - 1, pltpu.roll(after, rows - 1, 0), pltpu.roll(now, rows - 1, 0))
    return above, below


def multigrid(n_blk, core, b, scratch):
    step = 8
    ext, wide = scratch[1].shape
    sizes = [(ext >> d, wide >> d) for d in range(LEVELS)]
    names = ("visc", "fric", "f", "a", "b", "e", "w", "n", "s", "d", "i")
    lev = [dict(zip(names, scratch[d * len(names):(d + 1) * len(names)])) for d in range(LEVELS)]
    down, right, up, left = scratch[LEVELS * len(names):]

    def matrices():
        r, c = down.shape
        down[...] = jnp.where(iota((r, c), 1) // 2 == iota((r, c), 0), 0.25, 0.0).astype(BF16)
        r, c = up.shape
        up[...] = jnp.where(iota((r, c), 0) // 2 == iota((r, c), 1), 1.0, 0.0).astype(BF16)
        r, c = right.shape
        right[...] = jnp.where(iota((r, c), 0) // 2 == iota((r, c), 1), 1.0, 0.0).astype(BF16)
        r, c = left.shape
        left[...] = jnp.where(iota((r, c), 1) // 2 == iota((r, c), 0), 1.0, 0.0).astype(BF16)

    def panels(x, one):
        r, c = x.shape
        width = one.shape[0]
        count = c // width
        stacked = jnp.concatenate(
            [part[:, p * width:(p + 1) * width].astype(BF16)
             for part in split(x) for p in range(count)], axis=0)
        y = jnp.dot(stacked, one, preferred_element_type=F32)
        return jnp.concatenate(
            [y[p * r:(p + 1) * r] + y[(count + p) * r:(count + p + 1) * r] for p in range(count)],
            axis=1)

    def restrict(x):
        r, c = x.shape
        return dot2(panels(x, right[...]), down[:r // 2, :r], left=True)

    def prolong(x):
        r, c = x.shape
        return panels(dot2(x, up[:2 * r, :r], left=True), left[...])

    def chunks(d, body, trim=0):
        rows = sizes[d][0]
        low = (trim >> d) // step
        count = rows // step - 2 * low

        def run(index, carry):
            body(pl.multiple_of((index + low) * step, step))
            return carry

        lax.fori_loop(0, count, run, 0, unroll=count if d else 8 if count % 8 == 0 else 2)

    def neighbours(ref, at):
        now = ref[pl.ds(at + step, step), :]
        before = ref[pl.ds(at, step), :]
        after = ref[pl.ds(at + 2 * step, step), :]
        above, below = shift_rows(before, now, after)
        cols = now.shape[1]
        return now, above, below, pltpu.roll(now, 1, 1), pltpu.roll(now, cols - 1, 1)

    def coefficients():
        for d in range(LEVELS):
            m = lev[d]
            rows, cols = sizes[d]
            zero = jnp.zeros((step, cols), F32)
            for name in ("visc", "a", "b"):
                m[name][0:step, :] = zero
                m[name][rows + step:rows + 2 * step, :] = zero
            if d > 0:
                m["visc"][step:rows + step, :] = restrict(lev[d - 1]["visc"][step:2 * rows + step, :])
                m["fric"][...] = restrict(lev[d - 1]["fric"][...])
            halo = ext // 3 >> d
            low = jnp.where(jnp.logical_and(core == 0, b == 0), halo, 0)
            high = jnp.where(jnp.logical_and(core == 1, b == n_blk - 1), rows - halo, rows)
            scale = 0.5 * 0.25 ** d

            def faces(at, m=m, cols=cols, low=low, high=high, scale=scale):
                now, above, below, west, east = neighbours(m["visc"], at)
                col = iota(now.shape, 1)
                fe = scale * (now + below)
                fw = scale * (now + above)
                fn = scale * (now + jnp.where(col == cols - 1, 0.0, east))
                fs = scale * (now + jnp.where(col == 0, 0.0, west))
                here = pl.ds(at, step)
                diag = fe + fw + fn + fs + m["fric"][here, :]
                row = iota(now.shape, 0) + at
                inside = jnp.logical_and(row >= low, row < high)
                m["d"][here, :] = diag
                m["i"][here, :] = jnp.where(inside, omega / diag, 0.0)
                m["e"][here, :] = fe
                m["w"][here, :] = fw
                m["n"][here, :] = jnp.where(col == cols - 1, 0.0, fn)
                m["s"][here, :] = jnp.where(col == 0, 0.0, fs)

            chunks(d, faces)

    def flux(m, ref, at):
        now, above, below, west, east = neighbours(ref, at)
        here = pl.ds(at, step)
        total = (m["f"][here, :] + m["e"][here, :] * below + m["w"][here, :] * above
                 + m["n"][here, :] * east + m["s"][here, :] * west)
        return now, total

    def sweep(d, old, new, trim):
        m = lev[d]

        def body(at):
            now, total = flux(m, m[old], at)
            m[new][pl.ds(at + step, step), :] = (1.0 - omega) * now + m["i"][pl.ds(at, step), :] * total

        chunks(d, body, trim)

    def first(d, new, trim):
        m = lev[d]

        def body(at):
            here = pl.ds(at, step)
            m[new][pl.ds(at + step, step), :] = m["i"][here, :] * m["f"][here, :]

        chunks(d, body, trim)

    def residual(d, old, new, trim):
        m = lev[d]

        def body(at):
            now, total = flux(m, m[old], at)
            m[new][pl.ds(at + step, step), :] = total - m["d"][pl.ds(at, step), :] * now

        chunks(d, body, trim)

    def vcycle(d, zero, trim, after):
        m = lev[d]
        rows, cols = sizes[d]
        sweeps = COARSE_SWEEPS if d == LEVELS - 1 else SMOOTH_SWEEPS
        for index in range(sweeps):
            old, new = ("a", "b") if index % 2 == 0 else ("b", "a")
            if index == 0 and zero:
                first(d, new, trim)
            else:
                sweep(d, old, new, trim)
        if d == LEVELS - 1:
            return
        residual(d, "a", "b", trim)
        low, high = trim >> d, rows - (trim >> d)
        lev[d + 1]["f"][low // 2:high // 2, :] = restrict(m["b"][low + step:high + step, :])
        vcycle(d + 1, True, trim, trim)
        m["a"][low + step:high + step, :] += prolong(
            lev[d + 1]["a"][low // 2 + step:high // 2 + step, :])
        for index in range(SMOOTH_SWEEPS):
            old, new = ("a", "b") if index % 2 == 0 else ("b", "a")
            sweep(d, old, new, after)

    def cycles():
        inner = ext // 6
        for cycle_index in range(CYCLES):
            vcycle(0, cycle_index == 0, 0 if cycle_index < CYCLES - 1 else inner, inner)

    return lev[0], matrices, coefficients, cycles


def step_kernel(n_grp, n_blk, temp, uvel, vvel, col, cell, cav, thick, visc, fric, drive,
                temp_out, vel_out, ent_cell, ent_cav, ent_w, acc, drafts, dback, row_edge,
                col_edge, row_in, col_in, part, near, pair, far, esem_s, esem_r, hsem_s, hsem_r,
                bsem_s, bsem_r, zsem_s, zsem_r, gsem_s, gsem_r, psem_s, psem_r, osem_s, osem_r,
                sem_s, sem_r, *scratch):
    g = lax.axis_index("grp")
    b = lax.axis_index("blk")
    core = lax.rem(g, 2)
    z = g // 2
    nz = n_grp // 2
    rows, cols = thick.shape
    half = rows // 2
    size = half // nz
    count = cell.shape[1]
    levels, ocean_rows, ocean_cols = temp.shape
    up_g, dn_g = lax.rem(g + 1, n_grp), lax.rem(g + n_grp - 1, n_grp)
    up_b, dn_b = lax.rem(b + 1, n_blk), lax.rem(b + n_blk - 1, n_blk)
    partner = g + 1 - 2 * core
    outer = (partner, lax.rem(b + n_blk - 1 + 2 * core, n_blk))
    fine, matrices, coefficients, cycles = multigrid(n_blk, core, b, scratch)
    pad = 8

    def aligned(x):
        return pl.multiple_of(x, 8)

    barrier = pltpu.get_barrier_semaphore()
    peers = [(g, lax.rem(b + k, n_blk)) for k in range(1, n_blk)]
    bpeers = [(g, lax.rem(b + n_blk - k, n_blk)) for k in range(1, n_blk)]
    zpeers = [(lax.rem(g + 2 * k, n_grp), b) for k in range(1, nz)]
    greet = peers + [(up_g, b), (dn_g, b), (partner, b), outer] + zpeers
    for device in greet:
        pl.semaphore_signal(barrier, inc=1, device_id=device, device_id_type=MESH)
    at_lane = iota((ocean_rows, ocean_cols), 1)
    for side in range(2):
        edge = jnp.zeros((ocean_rows, ocean_cols), F32)
        r, c = (0, 0) if side == 0 else (ocean_rows - 1, ocean_cols - 1)
        for k in range(levels):
            row_edge[side, 0, k:k + 1, :] = temp[k, r:r + 1, :]
            row_edge[side, 1, k:k + 1, :] = uvel[k, r:r + 1, :]
            for which, ref in enumerate((temp, vvel)):
                lane = which * levels + k
                moved = pltpu.roll(ref[k], (lane - c) % ocean_cols, 1)
                edge = jnp.where(at_lane == lane, moved, edge)
        col_edge[side] = edge
    pl.semaphore_wait(barrier, len(greet))

    ent = []
    for k in range(1, n_blk):
        target = peers[k - 1]
        trio = [
            remote(cell, ent_cell.at[k - 1], esem_s.at[k - 1, 0], esem_r.at[k - 1, 0], target),
            remote(cav, ent_cav.at[k - 1], esem_s.at[k - 1, 1], esem_r.at[k - 1, 1], target),
            remote(ent_w.at[0], ent_w.at[k], esem_s.at[k - 1, 2], esem_r.at[k - 1, 2], target),
        ]
        trio[0].start()
        trio[1].start()
        ent.append(trio)

    ids = col[...]
    ocean_row = ids // ocean_cols
    ocean_lane = ids - ocean_row * ocean_cols
    pick = (iota((ocean_cols, count), 0) == ocean_lane).astype(F32).astype(BF16)
    surface = temp[0]
    rest = split(split(surface)[1])[1]
    wide = dot2(surface, pick) + jnp.dot(rest.astype(BF16), pick, preferred_element_type=F32)
    top = jnp.sum(jnp.where(iota((ocean_rows, count), 0) == ocean_row, wide, 0.0), axis=0,
                  keepdims=True)
    ent_w[0] = cav[...].astype(F32) * melt_rate * (top + 0.5)
    for trio in ent:
        trio[2].start()

    edges = [
        remote(row_edge.at[1], row_in.at[0], hsem_s.at[0], hsem_r.at[0], (up_g, b)),
        remote(row_edge.at[0], row_in.at[1], hsem_s.at[1], hsem_r.at[1], (dn_g, b)),
        remote(col_edge.at[1], col_in.at[0], hsem_s.at[2], hsem_r.at[2], (g, up_b)),
        remote(col_edge.at[0], col_in.at[1], hsem_s.at[3], hsem_r.at[3], (g, dn_b)),
    ]
    for copy in edges:
        copy.start()
    own = aligned((1 - core) * half)
    halo = aligned(core * 2 * half)
    target = (g, lax.rem(b + n_blk + 1 - 2 * core, n_blk))
    does = jnp.where(core == 0, b < n_blk - 1, b > 0)
    gets = jnp.where(core == 0, b > 0, b < n_blk - 1)
    ice = [
        remote(visc.at[pl.ds(own, half)], fine["visc"].at[pl.ds(halo + pad, half)], hsem_s.at[4],
               hsem_r.at[4], target),
        remote(fric.at[pl.ds(own, half)], fine["fric"].at[pl.ds(halo, half)], hsem_s.at[5],
               hsem_r.at[5], target),
    ]

    @pl.when(does)
    def _():
        for copy in ice:
            copy.start()

    fine["visc"][pl.ds(own + pad, 2 * half), :] = visc[...]
    fine["fric"][pl.ds(own, 2 * half), :] = fric[...]

    @pl.when(jnp.logical_not(gets))
    def _():
        fine["visc"][pl.ds(halo + pad, half), :] = jnp.zeros((half, cols), F32)
        fine["fric"][pl.ds(halo, half), :] = jnp.ones((half, cols), F32)

    high, low = split(thick[...])
    thick2 = jnp.concatenate([high, low], axis=0).astype(BF16)
    acc[...] = jnp.zeros_like(acc)
    chunk = min(512, count)
    for k in range(n_blk):
        if k > 0:
            for copy in ent[k - 1]:
                copy.wait_recv()
        cells_ref = cell if k == 0 else ent_cell.at[k - 1]
        cav_ref = cav if k == 0 else ent_cav.at[k - 1]

        for piece in range(count // chunk):
            at = slice(piece * chunk, (piece + 1) * chunk)
            cells = cells_ref[:, at]
            grid_row = cells // cols
            lane = cells - grid_row * cols
            hit = iota((rows, chunk), 0) == grid_row - b * rows
            pick = (iota((cols, chunk), 0) == lane).astype(F32).astype(BF16)
            found = jnp.dot(thick2, pick, preferred_element_type=F32)
            draft = jnp.sum(jnp.where(hit, found[:rows] + found[rows:], 0.0), axis=0, keepdims=True)
            drafts[k, :, at] = draft
            melt = ent_w[k, :, at] + cav_ref[:, at].astype(F32) * (0.5 * melt_rate) * draft
            m_high, m_low = split(melt)
            spread = jnp.concatenate(
                [jnp.where(hit, m_high, 0.0).astype(BF16), jnp.where(hit, m_low, 0.0).astype(BF16)],
                axis=0)
            acc[...] += nt(spread, pick)

    part[...] = acc[:rows] + acc[rows:]

    give = aligned((1 - core) * half)
    keep = aligned(core * half)
    first = remote(part.at[pl.ds(give, half)], pair, sem_s.at[0], sem_r.at[0], (partner, b))
    first.start()
    back = [
        remote(drafts.at[k], dback.at[k - 1], bsem_s.at[k - 1], bsem_r.at[k - 1], bpeers[k - 1])
        for k in range(1, n_blk)
    ]
    for copy in back:
        copy.start()
    matrices()
    first.wait_recv()
    near[...] = part[pl.ds(keep, half), :] + pair[...]

    scatter = []
    for k in range(1, nz):
        to = lax.rem(z + k, nz)
        copy = remote(near.at[pl.ds(aligned(to * size), size)], far.at[k - 1],
                      zsem_s.at[k - 1], zsem_r.at[k - 1], zpeers[k - 1])
        copy.start()
        scatter.append(copy)

    @pl.when(gets)
    def _():
        for copy in ice:
            copy.wait_recv()

    coefficients()

    source = fine["f"]
    mine = aligned(z * size)
    total = near[pl.ds(mine, size), :] + drive[pl.ds(aligned(core * half + z * size), size), :]
    for k in range(1, nz):
        scatter[k - 1].wait_recv()
        total = total + far[k - 1]
    source[pl.ds(aligned(half + z * size), size), :] = total

    there = core * 2 * half
    away = (1 - core) * 2 * half
    out_does = jnp.where(core == 0, b > 0, b < n_blk - 1)
    spread, swaps, outs = [], [], []
    for k in range(1, nz):
        block = source.at[pl.ds(aligned(half + z * size), size)]
        copy = remote(block, block, gsem_s.at[k - 1], gsem_r.at[k - 1], zpeers[k - 1])
        copy.start()
        spread.append(copy)

    def forward(k):
        at = lax.rem(z + nz - k, nz) * size
        block = source.at[pl.ds(aligned(half + at), size)]
        swap = remote(block, source.at[pl.ds(aligned(there + at), size)], psem_s.at[k],
                      psem_r.at[k], (partner, b))
        out = remote(block, source.at[pl.ds(aligned(away + at), size)], osem_s.at[k],
                     osem_r.at[k], outer)
        swap.start()
        swaps.append(swap)
        outs.append(out)

        @pl.when(out_does)
        def _():
            out.start()

    forward(0)

    @pl.when(jnp.logical_not(out_does))
    def _():
        source[pl.ds(aligned(there), half), :] = jnp.zeros((half, cols), F32)

    for copy in edges:
        copy.wait()
    draft = drafts[0]
    for k in range(1, n_blk):
        back[k - 1].wait_recv()
        draft = draft + dback[k - 1]
    for k in range(1, nz):
        spread[k - 1].wait_recv()
        forward(k)

    melt = ent_w[0] + cav[...].astype(F32) * (0.5 * melt_rate) * draft
    ocean(n_grp, n_blk, g, b, temp, uvel, vvel, row_in, col_in, col, melt, temp_out)

    for copy in swaps:
        copy.wait()

    @pl.when(out_does)
    def _():
        for copy in outs:
            copy.wait()

    cycles()

    here = aligned(core * half)
    block = fine["a"].at[pl.ds(half + pad, half)]
    last = remote(block, vel_out.at[pl.ds(here, half)], sem_s.at[1], sem_r.at[1], (partner, b))
    last.start()
    vel_out[pl.ds(here, half), :] = fine["a"][half + pad:2 * half + pad, :]
    for trio in ent:
        for copy in trio:
            copy.wait_send()

    @pl.when(does)
    def _():
        for copy in ice:
            copy.wait_send()

    first.wait_send()
    for copy in back + scatter + spread:
        copy.wait_send()
    last.wait()


def shards(n_grp, n_blk, temp, uvel, vvel, couple_col, couple_cell, cavity, thickness, viscosity,
           friction, drive):
    levels, orows, ocols = temp.shape
    rows, cols = thickness.shape
    half = rows // 2
    count = couple_col.shape[-1]
    nz = n_grp // 2
    ext = 3 * half
    scratch = []
    for depth in range(LEVELS):
        r, c = ext >> depth, cols >> depth
        tall, flat = pltpu.VMEM((r + 16, c), F32), pltpu.VMEM((r, c), F32)
        scratch += [tall, flat, flat, tall, tall] + [flat] * 6
    scratch += [pltpu.VMEM((ext // 2, ext), BF16), pltpu.VMEM((256, 128), BF16),
                pltpu.VMEM((ext, ext // 2), BF16), pltpu.VMEM((128, 256), BF16)]

    def pair_of(*dims):
        return [pltpu.SemaphoreType.DMA(dims)] * 2

    return pl.pallas_call(
        functools.partial(step_kernel, n_grp, n_blk),
        out_shape=(jax.ShapeDtypeStruct((levels, orows, ocols), F32),
                   jax.ShapeDtypeStruct((rows, cols), F32)),
        in_specs=[VM] * 10,
        out_specs=(VM,) * 2,
        scratch_shapes=[
            pltpu.VMEM((n_blk - 1, 1, count), jnp.int32),
            pltpu.VMEM((n_blk - 1, 1, count), jnp.int32),
            pltpu.VMEM((n_blk, 1, count), F32),
            pltpu.VMEM((2 * rows, cols), F32),
            pltpu.VMEM((n_blk, 1, count), F32),
            pltpu.VMEM((n_blk - 1, 1, count), F32),
            pltpu.VMEM((2, 2, levels, ocols), F32),
            pltpu.VMEM((2, orows, ocols), F32),
            pltpu.VMEM((2, 2, levels, ocols), F32),
            pltpu.VMEM((2, orows, ocols), F32),
            pltpu.VMEM((rows, cols), F32),
            pltpu.VMEM((half, cols), F32),
            pltpu.VMEM((half, cols), F32),
            pltpu.VMEM((nz - 1, half // nz, cols), F32),
        ] + pair_of(n_blk - 1, 3) + pair_of(6) + pair_of(n_blk - 1) + pair_of(nz - 1)
        + pair_of(nz - 1) + pair_of(nz) + pair_of(nz) + pair_of(2) + scratch,
        compiler_params=pltpu.CompilerParams(
            vmem_limit_bytes=LIMIT, collective_id=0, has_side_effects=True),
        name="step",
    )(temp, uvel, vvel, couple_col.reshape(1, count), couple_cell.reshape(1, count),
      cavity.reshape(1, count), thickness, viscosity, friction, drive)


def solution(mesh):
    sizes = dict(mesh.shape)
    return jax.shard_map(
        functools.partial(shards, sizes["grp"], sizes["blk"]),
        mesh=mesh,
        in_specs=(
            P(None, "grp", "blk"),
            P(None, "grp", "blk"),
            P(None, "grp", "blk"),
            P("grp", "blk", None),
            P("grp", "blk", None),
            P("grp", "blk", None),
            P("blk", None),
            P("blk", None),
            P("blk", None),
            P("blk", None),
        ),
        out_specs=(P(None, "grp", "blk"), P("blk", None)),
        check_vma=False,
    )
```

```python
import functools

import jax
import jax.numpy as jnp
from jax import lax
from jax.experimental import pallas as pl
from jax.experimental.pallas import tpu as pltpu
from jax.sharding import PartitionSpec as P

LEVELS = 3
SMOOTH_SWEEPS = 2
COARSE_SWEEPS = 4
CYCLES = 2

omega = 0.8
kappa = 0.1
vertical_mix = 0.2
melt_rate = 0.5

MESH = pl.DeviceIdType.MESH
VM = pl.BlockSpec(memory_space=pltpu.VMEM)
LIMIT = 56 * 1024 * 1024
F32 = jnp.float32
BF16 = jnp.bfloat16


def split(x):
    high = x.astype(BF16).astype(F32)
    return high, x - high


def dot2(x, one, left=False):
    out = None
    for part in split(x):
        part = part.astype(BF16)
        term = jnp.dot(one, part, preferred_element_type=F32) if left else jnp.dot(
            part, one, preferred_element_type=F32)
        out = term if out is None else out + term
    return out


def nt(a, b):
    return lax.dot_general(a, b, (((1,), (1,)), ((), ())), preferred_element_type=F32)


def iota(shape, dim):
    return lax.broadcasted_iota(jnp.int32, shape, dim)


def remote(src, dst, send, recv, device):
    return pltpu.make_async_remote_copy(
        src_ref=src, dst_ref=dst, send_sem=send, recv_sem=recv, device_id=device,
        device_id_type=MESH)


def ocean(n_grp, n_blk, g, b, temp, uvel, vvel, row_edge, col_edge, col, melt, out):
    levels, rows, cols = temp.shape
    count = col.shape[1]
    ids = col[...]
    row = ids // cols
    lane = ids - row * cols
    hit = iota((rows, count), 0) == row
    pick = (iota((cols, count), 0) == lane).astype(F32).astype(BF16)
    high, low = split(melt)
    surface = nt(jnp.where(hit, high, 0.0).astype(BF16), pick)
    surface = surface + nt(jnp.where(hit, low, 0.0).astype(BF16), pick)

    west_in = (g > 0).astype(F32)
    east_in = (g < n_grp - 1).astype(F32)
    south_in = (b > 0).astype(F32)
    north_in = (b < n_blk - 1).astype(F32)
    at_row = iota((rows, cols), 0)
    at_col = iota((rows, cols), 1)

    def four(x, which, rowwise, colwise, k):
        found = []
        if rowwise:
            low = row_edge[0, which, k:k + 1, :] * west_in
            high = row_edge[1, which, k:k + 1, :] * east_in
            found.append(jnp.where(at_row == rows - 1, high, pltpu.roll(x, rows - 1, 0)))
            found.append(jnp.where(at_row == 0, low, pltpu.roll(x, 1, 0)))
        if colwise:
            lane = which * levels + k
            low = col_edge[0, :, lane:lane + 1] * south_in
            high = col_edge[1, :, lane:lane + 1] * north_in
            found.append(jnp.where(at_col == cols - 1, high, pltpu.roll(x, cols - 1, 1)))
            found.append(jnp.where(at_col == 0, low, pltpu.roll(x, 1, 1)))
        return found

    for k in range(levels):
        t = temp[k]
        u = uvel[k]
        v = vvel[k]
        te, tw, tn, ts = four(t, 0, True, True, k)
        ue, uw = four(u, 1, True, False, k)
        vn, vs = four(v, 1, False, True, k)
        ue = 0.5 * (u + ue)
        uw = 0.5 * (u + uw)
        vn = 0.5 * (v + vn)
        vs = 0.5 * (v + vs)
        flux_east = jnp.maximum(ue, 0.0) * t + jnp.minimum(ue, 0.0) * te
        flux_west = jnp.maximum(uw, 0.0) * tw + jnp.minimum(uw, 0.0) * t
        flux_north = jnp.maximum(vn, 0.0) * t + jnp.minimum(vn, 0.0) * tn
        flux_south = jnp.maximum(vs, 0.0) * ts + jnp.minimum(vs, 0.0) * t
        laplace = te + tw + tn + ts - 4.0 * t
        vert = jnp.zeros_like(t)
        if k + 1 < levels:
            vert = vert + (temp[k + 1] - t)
        if k > 0:
            vert = vert - (t - temp[k - 1])
        new = (t + flux_west - flux_east + flux_south - flux_north + kappa * laplace
               + vertical_mix * vert)
        if k == 0:
            new = new - melt_rate * surface
        out[k] = new


def shift_rows(before, now, after):
    rows = now.shape[0]
    at = iota(now.shape, 0)
    above = jnp.where(at == 0, pltpu.roll(before, 1, 0), pltpu.roll(now, 1, 0))
    below = jnp.where(at == rows - 1, pltpu.roll(after, rows - 1, 0), pltpu.roll(now, rows - 1, 0))
    return above, below


def multigrid(n_blk, core, b, scratch):
    step = 8
    ext, wide = scratch[1].shape
    sizes = [(ext >> d, wide >> d) for d in range(LEVELS)]
    names = ("visc", "fric", "f", "a", "b", "e", "w", "n", "s", "d", "i")
    lev = [dict(zip(names, scratch[d * len(names):(d + 1) * len(names)])) for d in range(LEVELS)]
    down, right, up, left = scratch[LEVELS * len(names):]

    def matrices():
        r, c = down.shape
        down[...] = jnp.where(iota((r, c), 1) // 2 == iota((r, c), 0), 0.25, 0.0).astype(BF16)
        r, c = up.shape
        up[...] = jnp.where(iota((r, c), 0) // 2 == iota((r, c), 1), 1.0, 0.0).astype(BF16)
        r, c = right.shape
        right[...] = jnp.where(iota((r, c), 0) // 2 == iota((r, c), 1), 1.0, 0.0).astype(BF16)
        r, c = left.shape
        left[...] = jnp.where(iota((r, c), 1) // 2 == iota((r, c), 0), 1.0, 0.0).astype(BF16)

    def panels(x, one):
        r, c = x.shape
        width = one.shape[0]
        count = c // width
        stacked = jnp.concatenate(
            [part[:, p * width:(p + 1) * width].astype(BF16)
             for part in split(x) for p in range(count)], axis=0)
        y = jnp.dot(stacked, one, preferred_element_type=F32)
        return jnp.concatenate(
            [y[p * r:(p + 1) * r] + y[(count + p) * r:(count + p + 1) * r] for p in range(count)],
            axis=1)

    def restrict(x):
        r, c = x.shape
        return dot2(panels(x, right[...]), down[:r // 2, :r], left=True)

    def prolong(x):
        r, c = x.shape
        return panels(dot2(x, up[:2 * r, :r], left=True), left[...])

    def chunks(d, body, trim=0):
        rows = sizes[d][0]
        low = (trim >> d) // step
        count = rows // step - 2 * low

        def run(index, carry):
            body(pl.multiple_of((index + low) * step, step))
            return carry

        lax.fori_loop(0, count, run, 0, unroll=count if d else 8 if count % 8 == 0 else 2)

    def neighbours(ref, at):
        now = ref[pl.ds(at + step, step), :]
        before = ref[pl.ds(at, step), :]
        after = ref[pl.ds(at + 2 * step, step), :]
        above, below = shift_rows(before, now, after)
        cols = now.shape[1]
        return now, above, below, pltpu.roll(now, 1, 1), pltpu.roll(now, cols - 1, 1)

    def coefficients():
        for d in range(LEVELS):
            m = lev[d]
            rows, cols = sizes[d]
            zero = jnp.zeros((step, cols), F32)
            for name in ("visc", "a", "b"):
                m[name][0:step, :] = zero
                m[name][rows + step:rows + 2 * step, :] = zero
            if d > 0:
                m["visc"][step:rows + step, :] = restrict(lev[d - 1]["visc"][step:2 * rows + step, :])
                m["fric"][...] = restrict(lev[d - 1]["fric"][...])
            halo = ext // 3 >> d
            low = jnp.where(jnp.logical_and(core == 0, b == 0), halo, 0)
            high = jnp.where(jnp.logical_and(core == 1, b == n_blk - 1), rows - halo, rows)
            scale = 0.5 * 0.25 ** d

            def faces(at, m=m, cols=cols, low=low, high=high, scale=scale):
                now, above, below, west, east = neighbours(m["visc"], at)
                col = iota(now.shape, 1)
                fe = scale * (now + below)
                fw = scale * (now + above)
                fn = scale * (now + jnp.where(col == cols - 1, 0.0, east))
                fs = scale * (now + jnp.where(col == 0, 0.0, west))
                here = pl.ds(at, step)
                diag = fe + fw + fn + fs + m["fric"][here, :]
                row = iota(now.shape, 0) + at
                inside = jnp.logical_and(row >= low, row < high)
                m["d"][here, :] = diag
                m["i"][here, :] = jnp.where(inside, omega / diag, 0.0)
                m["e"][here, :] = fe
                m["w"][here, :] = fw
                m["n"][here, :] = jnp.where(col == cols - 1, 0.0, fn)
                m["s"][here, :] = jnp.where(col == 0, 0.0, fs)

            chunks(d, faces)

    def flux(m, ref, at):
        now, above, below, west, east = neighbours(ref, at)
        here = pl.ds(at, step)
        total = (m["f"][here, :] + m["e"][here, :] * below + m["w"][here, :] * above
                 + m["n"][here, :] * east + m["s"][here, :] * west)
        return now, total

    def sweep(d, old, new, trim):
        m = lev[d]

        def body(at):
            now, total = flux(m, m[old], at)
            m[new][pl.ds(at + step, step), :] = (1.0 - omega) * now + m["i"][pl.ds(at, step), :] * total

        chunks(d, body, trim)

    def first(d, new, trim):
        m = lev[d]

        def body(at):
            here = pl.ds(at, step)
            m[new][pl.ds(at + step, step), :] = m["i"][here, :] * m["f"][here, :]

        chunks(d, body, trim)

    def residual(d, old, new, trim):
        m = lev[d]

        def body(at):
            now, total = flux(m, m[old], at)
            m[new][pl.ds(at + step, step), :] = total - m["d"][pl.ds(at, step), :] * now

        chunks(d, body, trim)

    def vcycle(d, zero, trim, after):
        m = lev[d]
        rows, cols = sizes[d]
        sweeps = COARSE_SWEEPS if d == LEVELS - 1 else SMOOTH_SWEEPS
        for index in range(sweeps):
            old, new = ("a", "b") if index % 2 == 0 else ("b", "a")
            if index == 0 and zero:
                first(d, new, trim)
            else:
                sweep(d, old, new, trim)
        if d == LEVELS - 1:
            return
        residual(d, "a", "b", trim)
        low, high = trim >> d, rows - (trim >> d)
        lev[d + 1]["f"][low // 2:high // 2, :] = restrict(m["b"][low + step:high + step, :])
        vcycle(d + 1, True, trim, trim)
        m["a"][low + step:high + step, :] += prolong(
            lev[d + 1]["a"][low // 2 + step:high // 2 + step, :])
        for index in range(SMOOTH_SWEEPS):
            old, new = ("a", "b") if index % 2 == 0 else ("b", "a")
            sweep(d, old, new, after)

    def cycles():
        inner = ext // 6
        for cycle_index in range(CYCLES):
            vcycle(0, cycle_index == 0, 0 if cycle_index < CYCLES - 1 else inner, inner)

    return lev[0], matrices, coefficients, cycles


def step_kernel(n_grp, n_blk, temp, uvel, vvel, col, cell, cav, thick, visc, fric, drive,
                temp_out, vel_out, ent_cell, ent_cav, ent_w, acc, drafts, dback, row_edge,
                col_edge, row_in, col_in, part, near, pair, far, esem_s, esem_r, hsem_s, hsem_r,
                bsem_s, bsem_r, zsem_s, zsem_r, gsem_s, gsem_r, psem_s, psem_r, osem_s, osem_r,
                sem_s, sem_r, *scratch):
    g = lax.axis_index("grp")
    b = lax.axis_index("blk")
    core = lax.rem(g, 2)
    z = g // 2
    nz = n_grp // 2
    rows, cols = thick.shape
    half = rows // 2
    size = half // nz
    count = cell.shape[1]
    levels, ocean_rows, ocean_cols = temp.shape
    up_g, dn_g = lax.rem(g + 1, n_grp), lax.rem(g + n_grp - 1, n_grp)
    up_b, dn_b = lax.rem(b + 1, n_blk), lax.rem(b + n_blk - 1, n_blk)
    partner = g + 1 - 2 * core
    outer = (partner, lax.rem(b + n_blk - 1 + 2 * core, n_blk))
    fine, matrices, coefficients, cycles = multigrid(n_blk, core, b, scratch)
    pad = 8

    def aligned(x):
        return pl.multiple_of(x, 8)

    barrier = pltpu.get_barrier_semaphore()
    peers = [(g, lax.rem(b + k, n_blk)) for k in range(1, n_blk)]
    bpeers = [(g, lax.rem(b + n_blk - k, n_blk)) for k in range(1, n_blk)]
    zpeers = [(lax.rem(g + 2 * k, n_grp), b) for k in range(1, nz)]
    greet = peers + [(up_g, b), (dn_g, b), (partner, b), outer] + zpeers
    for device in greet:
        pl.semaphore_signal(barrier, inc=1, device_id=device, device_id_type=MESH)
    at_lane = iota((ocean_rows, ocean_cols), 1)
    for side in range(2):
        edge = jnp.zeros((ocean_rows, ocean_cols), F32)
        r, c = (0, 0) if side == 0 else (ocean_rows - 1, ocean_cols - 1)
        for k in range(levels):
            row_edge[side, 0, k:k + 1, :] = temp[k, r:r + 1, :]
            row_edge[side, 1, k:k + 1, :] = uvel[k, r:r + 1, :]
            for which, ref in enumerate((temp, vvel)):
                lane = which * levels + k
                moved = pltpu.roll(ref[k], (lane - c) % ocean_cols, 1)
                edge = jnp.where(at_lane == lane, moved, edge)
        col_edge[side] = edge
    pl.semaphore_wait(barrier, len(greet))

    ent = []
    for k in range(1, n_blk):
        target = peers[k - 1]
        trio = [
            remote(cell, ent_cell.at[k - 1], esem_s.at[k - 1, 0], esem_r.at[k - 1, 0], target),
            remote(cav, ent_cav.at[k - 1], esem_s.at[k - 1, 1], esem_r.at[k - 1, 1], target),
            remote(ent_w.at[0], ent_w.at[k], esem_s.at[k - 1, 2], esem_r.at[k - 1, 2], target),
        ]
        trio[0].start()
        trio[1].start()
        ent.append(trio)

    ids = col[...]
    ocean_row = ids // ocean_cols
    ocean_lane = ids - ocean_row * ocean_cols
    pick = (iota((ocean_cols, count), 0) == ocean_lane).astype(F32).astype(BF16)
    surface = temp[0]
    rest = split(split(surface)[1])[1]
    wide = dot2(surface, pick) + jnp.dot(rest.astype(BF16), pick, preferred_element_type=F32)
    top = jnp.sum(jnp.where(iota((ocean_rows, count), 0) == ocean_row, wide, 0.0), axis=0,
                  keepdims=True)
    ent_w[0] = cav[...].astype(F32) * melt_rate * (top + 0.5)
    for trio in ent:
        trio[2].start()

    edges = [
        remote(row_edge.at[1], row_in.at[0], hsem_s.at[0], hsem_r.at[0], (up_g, b)),
        remote(row_edge.at[0], row_in.at[1], hsem_s.at[1], hsem_r.at[1], (dn_g, b)),
        remote(col_edge.at[1], col_in.at[0], hsem_s.at[2], hsem_r.at[2], (g, up_b)),
        remote(col_edge.at[0], col_in.at[1], hsem_s.at[3], hsem_r.at[3], (g, dn_b)),
    ]
    for copy in edges:
        copy.start()
    own = aligned((1 - core) * half)
    halo = aligned(core * 2 * half)
    target = (g, lax.rem(b + n_blk + 1 - 2 * core, n_blk))
    does = jnp.where(core == 0, b < n_blk - 1, b > 0)
    gets = jnp.where(core == 0, b > 0, b < n_blk - 1)
    ice = [
        remote(visc.at[pl.ds(own, half)], fine["visc"].at[pl.ds(halo + pad, half)], hsem_s.at[4],
               hsem_r.at[4], target),
        remote(fric.at[pl.ds(own, half)], fine["fric"].at[pl.ds(halo, half)], hsem_s.at[5],
               hsem_r.at[5], target),
    ]

    @pl.when(does)
    def _():
        for copy in ice:
            copy.start()

    fine["visc"][pl.ds(own + pad, 2 * half), :] = visc[...]
    fine["fric"][pl.ds(own, 2 * half), :] = fric[...]

    @pl.when(jnp.logical_not(gets))
    def _():
        fine["visc"][pl.ds(halo + pad, half), :] = jnp.zeros((half, cols), F32)
        fine["fric"][pl.ds(halo, half), :] = jnp.ones((half, cols), F32)

    high, low = split(thick[...])
    thick2 = jnp.concatenate([high, low], axis=0).astype(BF16)
    acc[...] = jnp.zeros_like(acc)
    chunk = min(1024, count)
    for k in range(n_blk):
        if k > 0:
            for copy in ent[k - 1]:
                copy.wait_recv()
        cells_ref = cell if k == 0 else ent_cell.at[k - 1]
        cav_ref = cav if k == 0 else ent_cav.at[k - 1]

        for piece in range(count // chunk):
            at = slice(piece * chunk, (piece + 1) * chunk)
            cells = cells_ref[:, at]
            grid_row = cells // cols
            lane = cells - grid_row * cols
            hit = iota((rows, chunk), 0) == grid_row - b * rows
            pick = (iota((cols, chunk), 0) == lane).astype(F32).astype(BF16)
            found = jnp.dot(thick2, pick, preferred_element_type=F32)
            draft = jnp.sum(jnp.where(hit, found[:rows] + found[rows:], 0.0), axis=0, keepdims=True)
            drafts[k, :, at] = draft
            melt = ent_w[k, :, at] + cav_ref[:, at].astype(F32) * (0.5 * melt_rate) * draft
            m_high, m_low = split(melt)
            spread = jnp.concatenate(
                [jnp.where(hit, m_high, 0.0).astype(BF16), jnp.where(hit, m_low, 0.0).astype(BF16)],
                axis=0)
            acc[...] += nt(spread, pick)

    part[...] = acc[:rows] + acc[rows:]

    give = aligned((1 - core) * half)
    keep = aligned(core * half)
    first = remote(part.at[pl.ds(give, half)], pair, sem_s.at[0], sem_r.at[0], (partner, b))
    first.start()
    back = [
        remote(drafts.at[k], dback.at[k - 1], bsem_s.at[k - 1], bsem_r.at[k - 1], bpeers[k - 1])
        for k in range(1, n_blk)
    ]
    for copy in back:
        copy.start()
    matrices()
    first.wait_recv()
    near[...] = part[pl.ds(keep, half), :] + pair[...]

    scatter = []
    for k in range(1, nz):
        to = lax.rem(z + k, nz)
        copy = remote(near.at[pl.ds(aligned(to * size), size)], far.at[k - 1],
                      zsem_s.at[k - 1], zsem_r.at[k - 1], zpeers[k - 1])
        copy.start()
        scatter.append(copy)

    @pl.when(gets)
    def _():
        for copy in ice:
            copy.wait_recv()

    coefficients()

    source = fine["f"]
    mine = aligned(z * size)
    total = near[pl.ds(mine, size), :] + drive[pl.ds(aligned(core * half + z * size), size), :]
    for k in range(1, nz):
        scatter[k - 1].wait_recv()
        total = total + far[k - 1]
    source[pl.ds(aligned(half + z * size), size), :] = total

    there = core * 2 * half
    away = (1 - core) * 2 * half
    out_does = jnp.where(core == 0, b > 0, b < n_blk - 1)
    spread, swaps, outs = [], [], []
    for k in range(1, nz):
        block = source.at[pl.ds(aligned(half + z * size), size)]
        copy = remote(block, block, gsem_s.at[k - 1], gsem_r.at[k - 1], zpeers[k - 1])
        copy.start()
        spread.append(copy)

    def forward(k):
        at = lax.rem(z + nz - k, nz) * size
        block = source.at[pl.ds(aligned(half + at), size)]
        swap = remote(block, source.at[pl.ds(aligned(there + at), size)], psem_s.at[k],
                      psem_r.at[k], (partner, b))
        out = remote(block, source.at[pl.ds(aligned(away + at), size)], osem_s.at[k],
                     osem_r.at[k], outer)
        swap.start()
        swaps.append(swap)
        outs.append(out)

        @pl.when(out_does)
        def _():
            out.start()

    forward(0)

    @pl.when(jnp.logical_not(out_does))
    def _():
        source[pl.ds(aligned(there), half), :] = jnp.zeros((half, cols), F32)

    for copy in edges:
        copy.wait()
    draft = drafts[0]
    for k in range(1, n_blk):
        back[k - 1].wait_recv()
        draft = draft + dback[k - 1]
    for k in range(1, nz):
        spread[k - 1].wait_recv()
        forward(k)

    melt = ent_w[0] + cav[...].astype(F32) * (0.5 * melt_rate) * draft
    ocean(n_grp, n_blk, g, b, temp, uvel, vvel, row_in, col_in, col, melt, temp_out)

    for copy in swaps:
        copy.wait()

    @pl.when(out_does)
    def _():
        for copy in outs:
            copy.wait()

    cycles()

    here = aligned(core * half)
    block = fine["a"].at[pl.ds(half + pad, half)]
    last = remote(block, vel_out.at[pl.ds(here, half)], sem_s.at[1], sem_r.at[1], (partner, b))
    last.start()
    vel_out[pl.ds(here, half), :] = fine["a"][half + pad:2 * half + pad, :]
    for trio in ent:
        for copy in trio:
            copy.wait_send()

    @pl.when(does)
    def _():
        for copy in ice:
            copy.wait_send()

    first.wait_send()
    for copy in back + scatter + spread:
        copy.wait_send()
    last.wait()


def shards(n_grp, n_blk, temp, uvel, vvel, couple_col, couple_cell, cavity, thickness, viscosity,
           friction, drive):
    levels, orows, ocols = temp.shape
    rows, cols = thickness.shape
    half = rows // 2
    count = couple_col.shape[-1]
    nz = n_grp // 2
    ext = 3 * half
    scratch = []
    for depth in range(LEVELS):
        r, c = ext >> depth, cols >> depth
        tall, flat = pltpu.VMEM((r + 16, c), F32), pltpu.VMEM((r, c), F32)
        scratch += [tall, flat, flat, tall, tall] + [flat] * 6
    scratch += [pltpu.VMEM((ext // 2, ext), BF16), pltpu.VMEM((256, 128), BF16),
                pltpu.VMEM((ext, ext // 2), BF16), pltpu.VMEM((128, 256), BF16)]

    def pair_of(*dims):
        return [pltpu.SemaphoreType.DMA(dims)] * 2

    return pl.pallas_call(
        functools.partial(step_kernel, n_grp, n_blk),
        out_shape=(jax.ShapeDtypeStruct((levels, orows, ocols), F32),
                   jax.ShapeDtypeStruct((rows, cols), F32)),
        in_specs=[VM] * 10,
        out_specs=(VM,) * 2,
        scratch_shapes=[
            pltpu.VMEM((n_blk - 1, 1, count), jnp.int32),
            pltpu.VMEM((n_blk - 1, 1, count), jnp.int32),
            pltpu.VMEM((n_blk, 1, count), F32),
            pltpu.VMEM((2 * rows, cols), F32),
            pltpu.VMEM((n_blk, 1, count), F32),
            pltpu.VMEM((n_blk - 1, 1, count), F32),
            pltpu.VMEM((2, 2, levels, ocols), F32),
            pltpu.VMEM((2, orows, ocols), F32),
            pltpu.VMEM((2, 2, levels, ocols), F32),
            pltpu.VMEM((2, orows, ocols), F32),
            pltpu.VMEM((rows, cols), F32),
            pltpu.VMEM((half, cols), F32),
            pltpu.VMEM((half, cols), F32),
            pltpu.VMEM((nz - 1, half // nz, cols), F32),
        ] + pair_of(n_blk - 1, 3) + pair_of(6) + pair_of(n_blk - 1) + pair_of(nz - 1)
        + pair_of(nz - 1) + pair_of(nz) + pair_of(nz) + pair_of(2) + scratch,
        compiler_params=pltpu.CompilerParams(
            vmem_limit_bytes=LIMIT, collective_id=0, has_side_effects=True),
        name="step",
    )(temp, uvel, vvel, couple_col.reshape(1, count), couple_cell.reshape(1, count),
      cavity.reshape(1, count), thickness, viscosity, friction, drive)


def solution(mesh):
    sizes = dict(mesh.shape)
    return jax.shard_map(
        functools.partial(shards, sizes["grp"], sizes["blk"]),
        mesh=mesh,
        in_specs=(
            P(None, "grp", "blk"),
            P(None, "grp", "blk"),
            P(None, "grp", "blk"),
            P("grp", "blk", None),
            P("grp", "blk", None),
            P("grp", "blk", None),
            P("blk", None),
            P("blk", None),
            P("blk", None),
            P("blk", None),
        ),
        out_specs=(P(None, "grp", "blk"), P("blk", None)),
        check_vma=False,
    )
```

```python
import functools

import jax
import jax.numpy as jnp
from jax import lax
from jax.experimental import pallas as pl
from jax.experimental.pallas import tpu as pltpu
from jax.sharding import PartitionSpec as P

LEVELS = 3
SMOOTH_SWEEPS = 2
COARSE_SWEEPS = 4
CYCLES = 2

omega = 0.8
kappa = 0.1
vertical_mix = 0.2
melt_rate = 0.5

MESH = pl.DeviceIdType.MESH
VM = pl.BlockSpec(memory_space=pltpu.VMEM)
LIMIT = 56 * 1024 * 1024
F32 = jnp.float32
BF16 = jnp.bfloat16


def split(x):
    high = x.astype(BF16).astype(F32)
    return high, x - high


def dot2(x, one, left=False):
    out = None
    for part in split(x):
        part = part.astype(BF16)
        term = jnp.dot(one, part, preferred_element_type=F32) if left else jnp.dot(
            part, one, preferred_element_type=F32)
        out = term if out is None else out + term
    return out


def nt(a, b):
    return lax.dot_general(a, b, (((1,), (1,)), ((), ())), preferred_element_type=F32)


def iota(shape, dim):
    return lax.broadcasted_iota(jnp.int32, shape, dim)


def remote(src, dst, send, recv, device):
    return pltpu.make_async_remote_copy(
        src_ref=src, dst_ref=dst, send_sem=send, recv_sem=recv, device_id=device,
        device_id_type=MESH)


def ocean(n_grp, n_blk, g, b, temp, uvel, vvel, row_edge, col_edge, col, melt, out):
    levels, rows, cols = temp.shape
    count = col.shape[1]
    ids = col[...]
    row = ids // cols
    lane = ids - row * cols
    hit = iota((rows, count), 0) == row
    pick = (iota((cols, count), 0) == lane).astype(F32).astype(BF16)
    high, low = split(melt)
    surface = nt(jnp.where(hit, high, 0.0).astype(BF16), pick)
    surface = surface + nt(jnp.where(hit, low, 0.0).astype(BF16), pick)

    west_in = (g > 0).astype(F32)
    east_in = (g < n_grp - 1).astype(F32)
    south_in = (b > 0).astype(F32)
    north_in = (b < n_blk - 1).astype(F32)
    at_row = iota((rows, cols), 0)
    at_col = iota((rows, cols), 1)

    def four(x, which, rowwise, colwise, k):
        found = []
        if rowwise:
            low = row_edge[0, which, k:k + 1, :] * west_in
            high = row_edge[1, which, k:k + 1, :] * east_in
            found.append(jnp.where(at_row == rows - 1, high, pltpu.roll(x, rows - 1, 0)))
            found.append(jnp.where(at_row == 0, low, pltpu.roll(x, 1, 0)))
        if colwise:
            lane = which * levels + k
            low = col_edge[0, :, lane:lane + 1] * south_in
            high = col_edge[1, :, lane:lane + 1] * north_in
            found.append(jnp.where(at_col == cols - 1, high, pltpu.roll(x, cols - 1, 1)))
            found.append(jnp.where(at_col == 0, low, pltpu.roll(x, 1, 1)))
        return found

    for k in range(levels):
        t = temp[k]
        u = uvel[k]
        v = vvel[k]
        te, tw, tn, ts = four(t, 0, True, True, k)
        ue, uw = four(u, 1, True, False, k)
        vn, vs = four(v, 1, False, True, k)
        ue = 0.5 * (u + ue)
        uw = 0.5 * (u + uw)
        vn = 0.5 * (v + vn)
        vs = 0.5 * (v + vs)
        flux_east = jnp.maximum(ue, 0.0) * t + jnp.minimum(ue, 0.0) * te
        flux_west = jnp.maximum(uw, 0.0) * tw + jnp.minimum(uw, 0.0) * t
        flux_north = jnp.maximum(vn, 0.0) * t + jnp.minimum(vn, 0.0) * tn
        flux_south = jnp.maximum(vs, 0.0) * ts + jnp.minimum(vs, 0.0) * t
        laplace = te + tw + tn + ts - 4.0 * t
        vert = jnp.zeros_like(t)
        if k + 1 < levels:
            vert = vert + (temp[k + 1] - t)
        if k > 0:
            vert = vert - (t - temp[k - 1])
        new = (t + flux_west - flux_east + flux_south - flux_north + kappa * laplace
               + vertical_mix * vert)
        if k == 0:
            new = new - melt_rate * surface
        out[k] = new


def shift_rows(before, now, after):
    rows = now.shape[0]
    at = iota(now.shape, 0)
    above = jnp.where(at == 0, pltpu.roll(before, 1, 0), pltpu.roll(now, 1, 0))
    below = jnp.where(at == rows - 1, pltpu.roll(after, rows - 1, 0), pltpu.roll(now, rows - 1, 0))
    return above, below


def multigrid(n_blk, core, b, scratch):
    step = 8
    ext, wide = scratch[1].shape
    sizes = [(ext >> d, wide >> d) for d in range(LEVELS)]
    names = ("visc", "fric", "f", "a", "b", "e", "w", "n", "s", "d", "i")
    lev = [dict(zip(names, scratch[d * len(names):(d + 1) * len(names)])) for d in range(LEVELS)]
    down, right, up, left = scratch[LEVELS * len(names):]

    def matrices():
        r, c = down.shape
        down[...] = jnp.where(iota((r, c), 1) // 2 == iota((r, c), 0), 0.25, 0.0).astype(BF16)
        r, c = up.shape
        up[...] = jnp.where(iota((r, c), 0) // 2 == iota((r, c), 1), 1.0, 0.0).astype(BF16)
        r, c = right.shape
        right[...] = jnp.where(iota((r, c), 0) // 2 == iota((r, c), 1), 1.0, 0.0).astype(BF16)
        r, c = left.shape
        left[...] = jnp.where(iota((r, c), 1) // 2 == iota((r, c), 0), 1.0, 0.0).astype(BF16)

    def panels(x, one):
        r, c = x.shape
        width = one.shape[0]
        count = c // width
        stacked = jnp.concatenate(
            [part[:, p * width:(p + 1) * width].astype(BF16)
             for part in split(x) for p in range(count)], axis=0)
        y = jnp.dot(stacked, one, preferred_element_type=F32)
        return jnp.concatenate(
            [y[p * r:(p + 1) * r] + y[(count + p) * r:(count + p + 1) * r] for p in range(count)],
            axis=1)

    def restrict(x):
        r, c = x.shape
        return dot2(panels(x, right[...]), down[:r // 2, :r], left=True)

    def prolong(x):
        r, c = x.shape
        return panels(dot2(x, up[:2 * r, :r], left=True), left[...])

    def chunks(d, body, trim=0):
        rows = sizes[d][0]
        low = (trim >> d) // step
        count = rows // step - 2 * low

        def run(index, carry):
            body(pl.multiple_of((index + low) * step, step))
            return carry

        lax.fori_loop(0, count, run, 0, unroll=count if d else 8 if count % 8 == 0 else 2)

    def neighbours(ref, at):
        now = ref[pl.ds(at + step, step), :]
        before = ref[pl.ds(at, step), :]
        after = ref[pl.ds(at + 2 * step, step), :]
        above, below = shift_rows(before, now, after)
        cols = now.shape[1]
        return now, above, below, pltpu.roll(now, 1, 1), pltpu.roll(now, cols - 1, 1)

    def coefficients():
        for d in range(LEVELS):
            m = lev[d]
            rows, cols = sizes[d]
            zero = jnp.zeros((step, cols), F32)
            for name in ("visc", "a", "b"):
                m[name][0:step, :] = zero
                m[name][rows + step:rows + 2 * step, :] = zero
            if d > 0:
                m["visc"][step:rows + step, :] = restrict(lev[d - 1]["visc"][step:2 * rows + step, :])
                m["fric"][...] = restrict(lev[d - 1]["fric"][...])
            halo = ext // 3 >> d
            low = jnp.where(jnp.logical_and(core == 0, b == 0), halo, 0)
            high = jnp.where(jnp.logical_and(core == 1, b == n_blk - 1), rows - halo, rows)
            scale = 0.5 * 0.25 ** d

            def faces(at, m=m, cols=cols, low=low, high=high, scale=scale):
                now, above, below, west, east = neighbours(m["visc"], at)
                col = iota(now.shape, 1)
                fe = scale * (now + below)
                fw = scale * (now + above)
                fn = scale * (now + jnp.where(col == cols - 1, 0.0, east))
                fs = scale * (now + jnp.where(col == 0, 0.0, west))
                here = pl.ds(at, step)
                diag = fe + fw + fn + fs + m["fric"][here, :]
                row = iota(now.shape, 0) + at
                inside = jnp.logical_and(row >= low, row < high)
                m["d"][here, :] = diag
                m["i"][here, :] = jnp.where(inside, omega / diag, 0.0)
                m["e"][here, :] = fe
                m["w"][here, :] = fw
                m["n"][here, :] = jnp.where(col == cols - 1, 0.0, fn)
                m["s"][here, :] = jnp.where(col == 0, 0.0, fs)

            chunks(d, faces)

    def flux(m, ref, at):
        now, above, below, west, east = neighbours(ref, at)
        here = pl.ds(at, step)
        total = (m["f"][here, :] + m["e"][here, :] * below + m["w"][here, :] * above
                 + m["n"][here, :] * east + m["s"][here, :] * west)
        return now, total

    def sweep(d, old, new, trim):
        m = lev[d]

        def body(at):
            now, total = flux(m, m[old], at)
            m[new][pl.ds(at + step, step), :] = (1.0 - omega) * now + m["i"][pl.ds(at, step), :] * total

        chunks(d, body, trim)

    def first(d, new, trim):
        m = lev[d]

        def body(at):
            here = pl.ds(at, step)
            m[new][pl.ds(at + step, step), :] = m["i"][here, :] * m["f"][here, :]

        chunks(d, body, trim)

    def residual(d, old, new, trim):
        m = lev[d]

        def body(at):
            now, total = flux(m, m[old], at)
            m[new][pl.ds(at + step, step), :] = total - m["d"][pl.ds(at, step), :] * now

        chunks(d, body, trim)

    def vcycle(d, zero, trim, after):
        m = lev[d]
        rows, cols = sizes[d]
        sweeps = COARSE_SWEEPS if d == LEVELS - 1 else SMOOTH_SWEEPS
        for index in range(sweeps):
            old, new = ("a", "b") if index % 2 == 0 else ("b", "a")
            if index == 0 and zero:
                first(d, new, trim)
            else:
                sweep(d, old, new, trim)
        if d == LEVELS - 1:
            return
        residual(d, "a", "b", trim)
        low, high = trim >> d, rows - (trim >> d)
        lev[d + 1]["f"][low // 2:high // 2, :] = restrict(m["b"][low + step:high + step, :])
        vcycle(d + 1, True, trim, trim)
        m["a"][low + step:high + step, :] += prolong(
            lev[d + 1]["a"][low // 2 + step:high // 2 + step, :])
        for index in range(SMOOTH_SWEEPS):
            old, new = ("a", "b") if index % 2 == 0 else ("b", "a")
            sweep(d, old, new, after)

    def cycles():
        inner = ext // 6
        for cycle_index in range(CYCLES):
            vcycle(0, cycle_index == 0, 0 if cycle_index < CYCLES - 1 else inner, inner)

    return lev[0], matrices, coefficients, cycles


def step_kernel(n_grp, n_blk, temp, uvel, vvel, col, cell, cav, thick, visc, fric, drive,
                temp_out, vel_out, ent_cell, ent_cav, ent_w, acc, drafts, dback, row_edge,
                col_edge, row_in, col_in, part, near, pair, far, esem_s, esem_r, hsem_s, hsem_r,
                bsem_s, bsem_r, zsem_s, zsem_r, gsem_s, gsem_r, psem_s, psem_r, osem_s, osem_r,
                sem_s, sem_r, *scratch):
    g = lax.axis_index("grp")
    b = lax.axis_index("blk")
    core = lax.rem(g, 2)
    z = g // 2
    nz = n_grp // 2
    rows, cols = thick.shape
    half = rows // 2
    size = half // nz
    count = cell.shape[1]
    levels, ocean_rows, ocean_cols = temp.shape
    up_g, dn_g = lax.rem(g + 1, n_grp), lax.rem(g + n_grp - 1, n_grp)
    up_b, dn_b = lax.rem(b + 1, n_blk), lax.rem(b + n_blk - 1, n_blk)
    partner = g + 1 - 2 * core
    outer = (partner, lax.rem(b + n_blk - 1 + 2 * core, n_blk))
    fine, matrices, coefficients, cycles = multigrid(n_blk, core, b, scratch)
    pad = 8

    def aligned(x):
        return pl.multiple_of(x, 8)

    barrier = pltpu.get_barrier_semaphore()
    peers = [(g, lax.rem(b + k, n_blk)) for k in range(1, n_blk)]
    bpeers = [(g, lax.rem(b + n_blk - k, n_blk)) for k in range(1, n_blk)]
    zpeers = [(lax.rem(g + 2 * k, n_grp), b) for k in range(1, nz)]
    greet = peers + [(up_g, b), (dn_g, b), (partner, b), outer] + zpeers
    for device in greet:
        pl.semaphore_signal(barrier, inc=1, device_id=device, device_id_type=MESH)
    at_lane = iota((ocean_rows, ocean_cols), 1)
    for side in range(2):
        edge = jnp.zeros((ocean_rows, ocean_cols), F32)
        r, c = (0, 0) if side == 0 else (ocean_rows - 1, ocean_cols - 1)
        for k in range(levels):
            row_edge[side, 0, k:k + 1, :] = temp[k, r:r + 1, :]
            row_edge[side, 1, k:k + 1, :] = uvel[k, r:r + 1, :]
            for which, ref in enumerate((temp, vvel)):
                lane = which * levels + k
                moved = pltpu.roll(ref[k], (lane - c) % ocean_cols, 1)
                edge = jnp.where(at_lane == lane, moved, edge)
        col_edge[side] = edge
    pl.semaphore_wait(barrier, len(greet))

    ent = []
    for k in range(1, n_blk):
        target = peers[k - 1]
        trio = [
            remote(cell, ent_cell.at[k - 1], esem_s.at[k - 1, 0], esem_r.at[k - 1, 0], target),
            remote(cav, ent_cav.at[k - 1], esem_s.at[k - 1, 1], esem_r.at[k - 1, 1], target),
            remote(ent_w.at[0], ent_w.at[k], esem_s.at[k - 1, 2], esem_r.at[k - 1, 2], target),
        ]
        trio[0].start()
        trio[1].start()
        ent.append(trio)

    ids = col[...]
    ocean_row = ids // ocean_cols
    ocean_lane = ids - ocean_row * ocean_cols
    pick = (iota((ocean_cols, count), 0) == ocean_lane).astype(F32).astype(BF16)
    surface = temp[0]
    rest = split(split(surface)[1])[1]
    wide = dot2(surface, pick) + jnp.dot(rest.astype(BF16), pick, preferred_element_type=F32)
    top = jnp.sum(jnp.where(iota((ocean_rows, count), 0) == ocean_row, wide, 0.0), axis=0,
                  keepdims=True)
    ent_w[0] = cav[...].astype(F32) * melt_rate * (top + 0.5)
    for trio in ent:
        trio[2].start()

    edges = [
        remote(row_edge.at[1], row_in.at[0], hsem_s.at[0], hsem_r.at[0], (up_g, b)),
        remote(row_edge.at[0], row_in.at[1], hsem_s.at[1], hsem_r.at[1], (dn_g, b)),
        remote(col_edge.at[1], col_in.at[0], hsem_s.at[2], hsem_r.at[2], (g, up_b)),
        remote(col_edge.at[0], col_in.at[1], hsem_s.at[3], hsem_r.at[3], (g, dn_b)),
    ]
    for copy in edges:
        copy.start()
    own = aligned((1 - core) * half)
    halo = aligned(core * 2 * half)
    target = (g, lax.rem(b + n_blk + 1 - 2 * core, n_blk))
    does = jnp.where(core == 0, b < n_blk - 1, b > 0)
    gets = jnp.where(core == 0, b > 0, b < n_blk - 1)
    ice = [
        remote(visc.at[pl.ds(own, half)], fine["visc"].at[pl.ds(halo + pad, half)], hsem_s.at[4],
               hsem_r.at[4], target),
        remote(fric.at[pl.ds(own, half)], fine["fric"].at[pl.ds(halo, half)], hsem_s.at[5],
               hsem_r.at[5], target),
    ]

    @pl.when(does)
    def _():
        for copy in ice:
            copy.start()

    fine["visc"][pl.ds(own + pad, 2 * half), :] = visc[...]
    fine["fric"][pl.ds(own, 2 * half), :] = fric[...]

    @pl.when(jnp.logical_not(gets))
    def _():
        fine["visc"][pl.ds(halo + pad, half), :] = jnp.zeros((half, cols), F32)
        fine["fric"][pl.ds(halo, half), :] = jnp.ones((half, cols), F32)

    high, low = split(thick[...])
    thick2 = jnp.concatenate([high, low], axis=0).astype(BF16)
    acc[...] = jnp.zeros_like(acc)
    chunk = min(2048, count)
    for k in range(n_blk):
        if k > 0:
            for copy in ent[k - 1]:
                copy.wait_recv()
        cells_ref = cell if k == 0 else ent_cell.at[k - 1]
        cav_ref = cav if k == 0 else ent_cav.at[k - 1]

        for piece in range(count // chunk):
            at = slice(piece * chunk, (piece + 1) * chunk)
            cells = cells_ref[:, at]
            grid_row = cells // cols
            lane = cells - grid_row * cols
            hit = iota((rows, chunk), 0) == grid_row - b * rows
            pick = (iota((cols, chunk), 0) == lane).astype(F32).astype(BF16)
            found = jnp.dot(thick2, pick, preferred_element_type=F32)
            draft = jnp.sum(jnp.where(hit, found[:rows] + found[rows:], 0.0), axis=0, keepdims=True)
            drafts[k, :, at] = draft
            melt = ent_w[k, :, at] + cav_ref[:, at].astype(F32) * (0.5 * melt_rate) * draft
            m_high, m_low = split(melt)
            spread = jnp.concatenate(
                [jnp.where(hit, m_high, 0.0).astype(BF16), jnp.where(hit, m_low, 0.0).astype(BF16)],
                axis=0)
            acc[...] += nt(spread, pick)

    part[...] = acc[:rows] + acc[rows:]

    give = aligned((1 - core) * half)
    keep = aligned(core * half)
    first = remote(part.at[pl.ds(give, half)], pair, sem_s.at[0], sem_r.at[0], (partner, b))
    first.start()
    back = [
        remote(drafts.at[k], dback.at[k - 1], bsem_s.at[k - 1], bsem_r.at[k - 1], bpeers[k - 1])
        for k in range(1, n_blk)
    ]
    for copy in back:
        copy.start()
    matrices()
    first.wait_recv()
    near[...] = part[pl.ds(keep, half), :] + pair[...]

    scatter = []
    for k in range(1, nz):
        to = lax.rem(z + k, nz)
        copy = remote(near.at[pl.ds(aligned(to * size), size)], far.at[k - 1],
                      zsem_s.at[k - 1], zsem_r.at[k - 1], zpeers[k - 1])
        copy.start()
        scatter.append(copy)

    @pl.when(gets)
    def _():
        for copy in ice:
            copy.wait_recv()

    coefficients()

    source = fine["f"]
    mine = aligned(z * size)
    total = near[pl.ds(mine, size), :] + drive[pl.ds(aligned(core * half + z * size), size), :]
    for k in range(1, nz):
        scatter[k - 1].wait_recv()
        total = total + far[k - 1]
    source[pl.ds(aligned(half + z * size), size), :] = total

    there = core * 2 * half
    away = (1 - core) * 2 * half
    out_does = jnp.where(core == 0, b > 0, b < n_blk - 1)
    spread, swaps, outs = [], [], []
    for k in range(1, nz):
        block = source.at[pl.ds(aligned(half + z * size), size)]
        copy = remote(block, block, gsem_s.at[k - 1], gsem_r.at[k - 1], zpeers[k - 1])
        copy.start()
        spread.append(copy)

    def forward(k):
        at = lax.rem(z + nz - k, nz) * size
        block = source.at[pl.ds(aligned(half + at), size)]
        swap = remote(block, source.at[pl.ds(aligned(there + at), size)], psem_s.at[k],
                      psem_r.at[k], (partner, b))
        out = remote(block, source.at[pl.ds(aligned(away + at), size)], osem_s.at[k],
                     osem_r.at[k], outer)
        swap.start()
        swaps.append(swap)
        outs.append(out)

        @pl.when(out_does)
        def _():
            out.start()

    forward(0)

    @pl.when(jnp.logical_not(out_does))
    def _():
        source[pl.ds(aligned(there), half), :] = jnp.zeros((half, cols), F32)

    for copy in edges:
        copy.wait()
    draft = drafts[0]
    for k in range(1, n_blk):
        back[k - 1].wait_recv()
        draft = draft + dback[k - 1]
    for k in range(1, nz):
        spread[k - 1].wait_recv()
        forward(k)

    melt = ent_w[0] + cav[...].astype(F32) * (0.5 * melt_rate) * draft
    ocean(n_grp, n_blk, g, b, temp, uvel, vvel, row_in, col_in, col, melt, temp_out)

    for copy in swaps:
        copy.wait()

    @pl.when(out_does)
    def _():
        for copy in outs:
            copy.wait()

    cycles()

    here = aligned(core * half)
    block = fine["a"].at[pl.ds(half + pad, half)]
    last = remote(block, vel_out.at[pl.ds(here, half)], sem_s.at[1], sem_r.at[1], (partner, b))
    last.start()
    vel_out[pl.ds(here, half), :] = fine["a"][half + pad:2 * half + pad, :]
    for trio in ent:
        for copy in trio:
            copy.wait_send()

    @pl.when(does)
    def _():
        for copy in ice:
            copy.wait_send()

    first.wait_send()
    for copy in back + scatter + spread:
        copy.wait_send()
    last.wait()


def shards(n_grp, n_blk, temp, uvel, vvel, couple_col, couple_cell, cavity, thickness, viscosity,
           friction, drive):
    levels, orows, ocols = temp.shape
    rows, cols = thickness.shape
    half = rows // 2
    count = couple_col.shape[-1]
    nz = n_grp // 2
    ext = 3 * half
    scratch = []
    for depth in range(LEVELS):
        r, c = ext >> depth, cols >> depth
        tall, flat = pltpu.VMEM((r + 16, c), F32), pltpu.VMEM((r, c), F32)
        scratch += [tall, flat, flat, tall, tall] + [flat] * 6
    scratch += [pltpu.VMEM((ext // 2, ext), BF16), pltpu.VMEM((256, 128), BF16),
                pltpu.VMEM((ext, ext // 2), BF16), pltpu.VMEM((128, 256), BF16)]

    def pair_of(*dims):
        return [pltpu.SemaphoreType.DMA(dims)] * 2

    return pl.pallas_call(
        functools.partial(step_kernel, n_grp, n_blk),
        out_shape=(jax.ShapeDtypeStruct((levels, orows, ocols), F32),
                   jax.ShapeDtypeStruct((rows, cols), F32)),
        in_specs=[VM] * 10,
        out_specs=(VM,) * 2,
        scratch_shapes=[
            pltpu.VMEM((n_blk - 1, 1, count), jnp.int32),
            pltpu.VMEM((n_blk - 1, 1, count), jnp.int32),
            pltpu.VMEM((n_blk, 1, count), F32),
            pltpu.VMEM((2 * rows, cols), F32),
            pltpu.VMEM((n_blk, 1, count), F32),
            pltpu.VMEM((n_blk - 1, 1, count), F32),
            pltpu.VMEM((2, 2, levels, ocols), F32),
            pltpu.VMEM((2, orows, ocols), F32),
            pltpu.VMEM((2, 2, levels, ocols), F32),
            pltpu.VMEM((2, orows, ocols), F32),
            pltpu.VMEM((rows, cols), F32),
            pltpu.VMEM((half, cols), F32),
            pltpu.VMEM((half, cols), F32),
            pltpu.VMEM((nz - 1, half // nz, cols), F32),
        ] + pair_of(n_blk - 1, 3) + pair_of(6) + pair_of(n_blk - 1) + pair_of(nz - 1)
        + pair_of(nz - 1) + pair_of(nz) + pair_of(nz) + pair_of(2) + scratch,
        compiler_params=pltpu.CompilerParams(
            vmem_limit_bytes=LIMIT, collective_id=0, has_side_effects=True),
        name="step",
    )(temp, uvel, vvel, couple_col.reshape(1, count), couple_cell.reshape(1, count),
      cavity.reshape(1, count), thickness, viscosity, friction, drive)


def solution(mesh):
    sizes = dict(mesh.shape)
    return jax.shard_map(
        functools.partial(shards, sizes["grp"], sizes["blk"]),
        mesh=mesh,
        in_specs=(
            P(None, "grp", "blk"),
            P(None, "grp", "blk"),
            P(None, "grp", "blk"),
            P("grp", "blk", None),
            P("grp", "blk", None),
            P("grp", "blk", None),
            P("blk", None),
            P("blk", None),
            P("blk", None),
            P("blk", None),
        ),
        out_specs=(P(None, "grp", "blk"), P("blk", None)),
        check_vma=False,
    )
```
